256 devices in a mesh: band: 64 (over z, x, core), chan: 4 (over y).
Axes of the slice: x: 4, y: 4, z: 8, core: 2. Of those that a mesh axis runs over, the one named last changes fastest.
Arguments:
- mesh_node_state: bfloat16 [8192, 1024], P('band'), may hold values from -6 to 6
- grid_state: bfloat16 [32768, 1024], P('band'), may hold values from -6 to 6
- d_out: bfloat16 [32768, 1024], P('band'), may hold values from -16 to 16
- neighbours: int32 [32768, 4], P('band'), may hold values from 0 to 8191, as said below
- edge_count: int32 [32768], P('band'), may hold values from 1 to 4
- w_proc_qkv: bfloat16 [3, 1024, 1024], P(None, None, 'chan')
- w_proc_out: bfloat16 [1024, 1024], P('chan'), may hold values from -0.1875 to 0.1875
- w_dec_q: bfloat16 [1024, 1024], P(None, 'chan'), may hold values from -0.1875 to 0.1875
- w_dec_kv: bfloat16 [2, 1024, 1024], P(None, None, 'chan'), may hold values from -0.1875 to 0.1875
- w_dec_out: bfloat16 [1024, 1024], P('chan'), may hold values from -0.1875 to 0.1875
Outputs:
- mesh_state_gradient: bfloat16 [8192, 1024], P('band')
- d_grid: bfloat16 [32768, 1024], P('band', 'chan')
- g_proc_qkv: float32 [3, 1024, 1024], P(None, 'band', 'chan')
- g_proc_out: float32 [1024, 1024], P('chan', 'band')
- g_dec_q: float32 [1024, 1024], P('band', 'chan')
- g_dec_kv: float32 [2, 1024, 1024], P(None, 'band', 'chan')
- g_dec_out: float32 [1024, 1024], P('chan', 'band')
The draws below stay inside these ranges and needn't reach their ends.
Inputs may be any that keep to these rules, and one draw needn't show every extreme that they name: `neighbours`: grid points of rows b*512 to (b+1)*512 - 1 list only mesh nodes of rows b*128 - 8 to (b+1)*128 + 7.
All inputs are finite; a program needn't handle non-finite values.
Results may differ from the reference program's by a relative error of at most 0.03.
Values may be sent and summed in bfloat16 or wider, within the bound.
A program may use at most 128 MiB of HBM per device.

```python
import jax
import jax.numpy as jnp
from jax import lax

D = 1024
HEADS = 16
HEAD_DIM = 64
EDGES = 4
REACH = 8
MESH_DEV = 128
GRID_DEV = 512
WINDOW = 128
MESH = 8192
GRID = 32768
N_BAND = 64


def draw_neighbours(key, part):
    row_index = jnp.arange(GRID, dtype=jnp.int32)
    band_index = row_index // GRID_DEV
    centre = band_index * MESH_DEV + row_index % GRID_DEV * MESH_DEV // GRID_DEV
    offset = jax.random.randint(key, (GRID, EDGES), -REACH, REACH + 1, dtype=jnp.int32)
    return jnp.clip(centre[:, None] + offset, 0, MESH - 1)


def draw_w_proc_qkv(key, part):
    parts_keys = jax.random.split(jax.random.fold_in(key, 17), 1)
    shape = (3, D, D)
    result = jax.random.normal(parts_keys[0], shape, jnp.float32) * D ** (-0.5)
    return result.astype(jnp.bfloat16)


def place_ends(values, key, smallest, largest):
    longest = values.shape.index(max(values.shape))
    spots = []
    for shift in (0, 1):
        where = [jax.random.randint(jax.random.fold_in(key, axis), (), 0, length) for axis, length in enumerate(values.shape)]
        where[longest] = (where[longest] + shift) % values.shape[longest]
        spots.append(tuple(where))
    return values.at[spots[0]].set(smallest).at[spots[1]].set(largest)


def with_spikes(values, rng, source, target, parts, factor):
    owner, partner = [(jnp.arange(values.shape[dim]) // (values.shape[dim] // parts)).reshape([-1 if axis == dim else 1 for axis in range(values.ndim)]) for dim in (source, target)]
    chosen = jax.random.permutation(rng, parts)[partner]
    strong = (owner == chosen) | (owner == (partner + parts // 2) % parts)
    return jnp.where(strong, factor * values, values)


def levels(stream_key, dims, shards, smallest, top_value):
    def one(axis_at, parts):
        steps = jax.random.uniform(jax.random.fold_in(jax.random.fold_in(stream_key, 6), axis_at), (parts,), jnp.float32, smallest / len(shards), top_value / len(shards))
        return jnp.repeat(jnp.exp(steps), dims[axis_at] // parts).reshape((-1,) + (1,) * (len(dims) - axis_at - 1))

    level = one(*shards[0])
    for cut in shards[1:]:
        level = level * one(*cut)
    return level


def normal_values(stream_key, shape, width, reach, cuts=(), kind=jnp.bfloat16):
    values = jax.random.normal(stream_key, shape, jnp.float32) * width
    if len(cuts) > 0:
        values = levels(stream_key, shape, cuts, -0.22, 0.18) * values
    return jnp.clip(values, min=-reach, max=reach).astype(kind)


def heavy_noise(stream_key, dims, scale, bound, pieces, heavy, held_as=jnp.bfloat16):
    values = scale * jax.random.normal(stream_key, dims, jnp.float32)
    if pieces:
        values = values * levels(stream_key, dims, pieces, -0.22, 0.18)
    return jnp.clip(with_spikes(values, jax.random.fold_in(stream_key, 3), *heavy), -bound, bound).astype(held_as)


def setup_inputs(seed: int = 0) -> dict:
    seeds = jax.random.split(jax.random.key(seed), 11)
    mesh_node_state = normal_values(seeds[0], (MESH, D), 1.0, 6.0, ((0, 64),))
    grid_state = normal_values(seeds[1], (GRID, D), 1.0, 6.0, ((0, 64),))
    d_out = heavy_noise(seeds[2], (GRID, D), 1.0, 16.0, ((0, 64),), (0, 1, 64, 4.0))
    neighbours = draw_neighbours(jax.random.fold_in(seeds[10], 71), 0)
    edge_count = place_ends(jax.random.randint(seeds[4], (GRID,), 1, EDGES + 1), jax.random.fold_in(seeds[4], 1), 1, EDGES).astype(jnp.int32)
    w_proc_qkv = draw_w_proc_qkv(jax.random.fold_in(seeds[10], 71), 0)
    w_proc_out = normal_values(seeds[6], (D, D), D ** -0.5, 0.1875, ((0, 4),))
    w_dec_q = normal_values(seeds[7], (D, D), D ** -0.5, 0.1875, ((1, 4),))
    w_dec_kv = normal_values(seeds[8], (2, D, D), D ** -0.5, 0.1875, ((2, 4),))
    w_dec_out = normal_values(seeds[9], (D, D), D ** -0.5, 0.1875, ((0, 4),))
    return dict(mesh_node_state=mesh_node_state, grid_state=grid_state, d_out=d_out, neighbours=neighbours, edge_count=edge_count, w_proc_qkv=w_proc_qkv, w_proc_out=w_proc_out, w_dec_q=w_dec_q, w_dec_kv=w_dec_kv, w_dec_out=w_dec_out)


EPS = 1e-05
NEG = -1e+30

def layer_norm_forward(values):
    values = values.astype(jnp.float32)
    centre = lax.optimization_barrier(jnp.mean(values, axis=-1, keepdims=True))
    shifted = values - centre
    rstd = lax.rsqrt(lax.optimization_barrier(jnp.mean(shifted * shifted, axis=-1, keepdims=True)) + EPS)
    return (shifted * rstd, rstd)

def layer_norm_backward(normed, rstd, upstream):
    first = lax.optimization_barrier(jnp.mean(upstream, axis=-1, keepdims=True))
    second = lax.optimization_barrier(jnp.mean(upstream * normed, axis=-1, keepdims=True))
    return rstd * (upstream - first - normed * second)

def back_dot(left, weight):
    return lax.dot_general(left, weight, (((1,), (1,)), ((), ())), preferred_element_type=jnp.float32)

def outer_sum(left, right):
    return lax.dot_general(left, right, (((0,), (0,)), ((), ())), preferred_element_type=jnp.float32)

def window_probs(query, keys, base_row, total_rows):
    row_count = query.shape[0]
    head_count = query.shape[1] // HEAD_DIM
    query_heads = query.astype(jnp.float32).reshape(row_count, head_count, HEAD_DIM)
    key_heads = keys.astype(jnp.float32).reshape(keys.shape[0], head_count, HEAD_DIM)
    scores = jnp.einsum('qhd,khd->hqk', query_heads, key_heads) * HEAD_DIM ** (-0.5)
    query_pos = base_row + jnp.arange(row_count, dtype=jnp.int32)
    key_pos = base_row - row_count + jnp.arange(keys.shape[0], dtype=jnp.int32)
    distance = query_pos[:, None] - key_pos[None, :]
    valid_pair = (jnp.abs(distance) <= WINDOW) & (key_pos[None, :] >= 0) & (key_pos[None, :] < total_rows)
    scores = jnp.where(valid_pair[None], scores, NEG)
    return jax.nn.softmax(scores, axis=-1)

def edge_pass(query, keys, values, local, count, upstream):
    row_count = query.shape[0]
    head_count = query.shape[1] // HEAD_DIM
    factor = HEAD_DIM ** (-0.5)
    query_heads = query.astype(jnp.float32).reshape(row_count, head_count, HEAD_DIM)
    keys_at = [keys[local[:, j]].astype(jnp.float32).reshape(row_count, head_count, HEAD_DIM) for j in range(EDGES)]
    values_at = [values[local[:, j]].astype(jnp.float32).reshape(row_count, head_count, HEAD_DIM) for j in range(EDGES)]
    scores = jnp.stack([lax.optimization_barrier(jnp.sum(query_heads * item, axis=-1)) for item in keys_at], axis=-1) * factor
    valid_edge = (jnp.arange(EDGES, dtype=jnp.int32)[None, :] < count[:, None])[:, None, :]
    scores = jnp.where(valid_edge, scores, NEG)
    weights = jax.nn.softmax(scores, axis=-1)
    output = weights[..., 0:1] * values_at[0]
    for j in range(1, EDGES):
        output = output + weights[..., j:j + 1] * values_at[j]
    up_heads = upstream.reshape(row_count, head_count, HEAD_DIM)
    dweight = jnp.stack([lax.optimization_barrier(jnp.sum(up_heads * item, axis=-1)) for item in values_at], axis=-1)
    dscore = weights * (dweight - lax.optimization_barrier(jnp.sum(weights * dweight, axis=-1, keepdims=True)))
    dquery = dscore[..., 0:1] * keys_at[0]
    for j in range(1, EDGES):
        dquery = dquery + dscore[..., j:j + 1] * keys_at[j]
    dquery = dquery * factor
    key_terms = jnp.stack([dscore[..., j:j + 1] * query_heads * factor for j in range(EDGES)], axis=0)
    value_terms = jnp.stack([weights[..., j:j + 1] * up_heads for j in range(EDGES)], axis=0)
    segment_ids = jnp.transpose(local).reshape(-1)
    dkeys = jax.ops.segment_sum(key_terms.reshape(EDGES * row_count, -1), segment_ids, num_segments=keys.shape[0])
    dvalues = jax.ops.segment_sum(value_terms.reshape(EDGES * row_count, -1), segment_ids, num_segments=keys.shape[0])
    return (output.reshape(row_count, -1), dquery.reshape(row_count, -1), dkeys, dvalues)

def fold_rims(extended, rim):
    middle = extended[:, :, rim:rim + MESH_DEV]
    lower = extended[:, :, :rim]
    upper = extended[:, :, rim + MESH_DEV:]
    zero_rim = jnp.zeros_like(lower[:, :1])
    from_above = jnp.concatenate([lower[:, 1:], zero_rim], axis=1)
    from_below = jnp.concatenate([zero_rim, upper[:, :-1]], axis=1)
    middle = middle.at[:, :, MESH_DEV - rim:].add(from_above)
    middle = middle.at[:, :, :rim].add(from_below)
    return middle

def reference(mesh_node_state, grid_state, d_out, neighbours, edge_count, w_proc_qkv, w_proc_out, w_dec_q, w_dec_kv, w_dec_out):
    brain_float_sixteen = jnp.bfloat16
    input_centred_scaled, inverse_deviation_input = layer_norm_forward(mesh_node_state)
    mesh_state_normalised = input_centred_scaled.astype(brain_float_sixteen)
    query_p = jnp.dot(mesh_state_normalised, w_proc_qkv[0], preferred_element_type=jnp.float32).astype(brain_float_sixteen)
    key_p = jnp.dot(mesh_state_normalised, w_proc_qkv[1], preferred_element_type=jnp.float32).astype(brain_float_sixteen)
    value_p = jnp.dot(mesh_state_normalised, w_proc_qkv[2], preferred_element_type=jnp.float32).astype(brain_float_sixteen)
    padding = ((MESH_DEV, MESH_DEV), (0, 0))
    key_pad = jnp.pad(key_p, padding)
    value_pad = jnp.pad(value_p, padding)
    block_ids = jnp.arange(N_BAND, dtype=jnp.int32)
    factor = HEAD_DIM ** (-0.5)

    def forward_block(index):
        base_row = index * MESH_DEV
        query = lax.dynamic_slice_in_dim(query_p, base_row, MESH_DEV, 0)
        keys = lax.dynamic_slice_in_dim(key_pad, base_row, 3 * MESH_DEV, 0)
        values = lax.dynamic_slice_in_dim(value_pad, base_row, 3 * MESH_DEV, 0)
        probs = window_probs(query, keys, base_row, MESH)
        probs_b = lax.optimization_barrier(probs.astype(brain_float_sixteen)).astype(jnp.float32)
        value_heads = values.astype(jnp.float32).reshape(3 * MESH_DEV, HEADS, HEAD_DIM)
        mixed = jnp.einsum('hqk,khd->qhd', probs_b, value_heads)
        return mixed.reshape(MESH_DEV, D).astype(brain_float_sixteen)
    attended = lax.map(forward_block, block_ids).reshape(MESH, D)
    state_out = (mesh_node_state.astype(jnp.float32) + jnp.dot(attended, w_proc_out, preferred_element_type=jnp.float32)).astype(brain_float_sixteen)
    yhat, rstd_y = layer_norm_forward(state_out)
    state_normed = yhat.astype(brain_float_sixteen)
    key_d = jnp.dot(state_normed, w_dec_kv[0], preferred_element_type=jnp.float32).astype(brain_float_sixteen)
    value_d = jnp.dot(state_normed, w_dec_kv[1], preferred_element_type=jnp.float32).astype(brain_float_sixteen)
    ghat, rstd_g = layer_norm_forward(grid_state)
    grid_normed = ghat.astype(brain_float_sixteen)
    query_d = jnp.dot(grid_normed, w_dec_q, preferred_element_type=jnp.float32).astype(brain_float_sixteen)
    upstream = back_dot(d_out, w_dec_out)
    rim_pad = ((REACH, REACH), (0, 0))
    key_d_pad = jnp.pad(key_d, rim_pad)
    value_d_pad = jnp.pad(value_d, rim_pad)

    def band_edges(index):
        grid_base = index * GRID_DEV
        mesh_base = index * MESH_DEV
        query = lax.dynamic_slice_in_dim(query_d, grid_base, GRID_DEV, 0)
        keys = lax.dynamic_slice_in_dim(key_d_pad, mesh_base, MESH_DEV + 2 * REACH, 0)
        values = lax.dynamic_slice_in_dim(value_d_pad, mesh_base, MESH_DEV + 2 * REACH, 0)
        local = lax.dynamic_slice_in_dim(neighbours, grid_base, GRID_DEV, 0) - mesh_base + REACH
        count = lax.dynamic_slice_in_dim(edge_count, grid_base, GRID_DEV, 0)
        upper = lax.dynamic_slice_in_dim(upstream, grid_base, GRID_DEV, 0)
        output, dquery_blk, dkeys, dvalues = edge_pass(query, keys, values, local, count, upper)
        return (output, dquery_blk, jnp.stack([dkeys, dvalues]))
    dec_out, dquery, dkv_dec = lax.map(band_edges, block_ids)
    dec_out = dec_out.reshape(GRID, D).astype(brain_float_sixteen)
    dquery = dquery.reshape(GRID, D).astype(brain_float_sixteen)
    dkv_dec = jnp.transpose(fold_rims(jnp.transpose(dkv_dec, (1, 0, 2, 3)), REACH), (0, 1, 2, 3))
    dkv_dec = dkv_dec.reshape(2, MESH, D).astype(brain_float_sixteen)
    dkey_d = dkv_dec[0]
    dvalue_d = dkv_dec[1]
    g_dec_out = outer_sum(dec_out, d_out)
    g_dec_q = outer_sum(grid_normed, dquery)
    g_dec_kv = jnp.stack([outer_sum(state_normed, dkey_d), outer_sum(state_normed, dvalue_d)])
    grid_back = back_dot(dquery, w_dec_q)
    d_grid = (d_out.astype(jnp.float32) + layer_norm_backward(ghat, rstd_g, grid_back)).astype(brain_float_sixteen)
    state_back = back_dot(dkey_d, w_dec_kv[0]) + back_dot(dvalue_d, w_dec_kv[1])
    state_gradient_value = layer_norm_backward(yhat, rstd_y, state_back)
    state_grad_b = state_gradient_value.astype(brain_float_sixteen)
    g_proc_out = outer_sum(attended, state_grad_b)
    dattended = back_dot(state_grad_b, w_proc_out).astype(brain_float_sixteen)

    def backward_block(index):
        base_row = index * MESH_DEV
        query = lax.dynamic_slice_in_dim(query_p, base_row, MESH_DEV, 0)
        keys = lax.dynamic_slice_in_dim(key_pad, base_row, 3 * MESH_DEV, 0)
        values = lax.dynamic_slice_in_dim(value_pad, base_row, 3 * MESH_DEV, 0)
        probs = window_probs(query, keys, base_row, MESH)
        probs_b = lax.optimization_barrier(probs.astype(brain_float_sixteen)).astype(jnp.float32)
        grad_heads = lax.dynamic_slice_in_dim(dattended, base_row, MESH_DEV, 0).astype(jnp.float32).reshape(MESH_DEV, HEADS, HEAD_DIM)
        query_heads = query.astype(jnp.float32).reshape(MESH_DEV, HEADS, HEAD_DIM)
        key_heads = keys.astype(jnp.float32).reshape(3 * MESH_DEV, HEADS, HEAD_DIM)
        value_heads = values.astype(jnp.float32).reshape(3 * MESH_DEV, HEADS, HEAD_DIM)
        dvalue_ext = jnp.einsum('hqk,qhd->khd', probs_b, grad_heads)
        dprob = jnp.einsum('qhd,khd->hqk', grad_heads, value_heads)
        centre = lax.optimization_barrier(jnp.sum(probs * dprob, axis=-1, keepdims=True))
        dscore = lax.optimization_barrier((probs * (dprob - centre)).astype(brain_float_sixteen)).astype(jnp.float32)
        dquery_blk = jnp.einsum('hqk,khd->qhd', dscore, key_heads) * factor
        dkey_ext = jnp.einsum('hqk,qhd->khd', dscore, query_heads) * factor
        return (dquery_blk.reshape(MESH_DEV, D), jnp.stack([dkey_ext, dvalue_ext]).reshape(2, 3 * MESH_DEV, D))
    dquery_blocks, dkv_blocks = lax.map(backward_block, block_ids)
    middle = dkv_blocks[:, :, MESH_DEV:2 * MESH_DEV]
    lower = dkv_blocks[:, :, :MESH_DEV]
    upper = dkv_blocks[:, :, 2 * MESH_DEV:]
    zero_block = jnp.zeros_like(middle[:1])
    own = middle + jnp.concatenate([lower[1:], zero_block], axis=0) + jnp.concatenate([zero_block, upper[:-1]], axis=0)
    dkv = jnp.transpose(own, (1, 0, 2, 3)).reshape(2, MESH, D).astype(brain_float_sixteen)
    dquery_p = dquery_blocks.reshape(MESH, D).astype(brain_float_sixteen)
    dkey_p = dkv[0]
    dvalue_p = dkv[1]
    g_proc_qkv = jnp.stack([outer_sum(mesh_state_normalised, dquery_p), outer_sum(mesh_state_normalised, dkey_p), outer_sum(mesh_state_normalised, dvalue_p)])
    mesh_backward_result = back_dot(dquery_p, w_proc_qkv[0]) + back_dot(dkey_p, w_proc_qkv[1]) + back_dot(dvalue_p, w_proc_qkv[2])
    mesh_state_gradient = (state_gradient_value + layer_norm_backward(input_centred_scaled, inverse_deviation_input, mesh_backward_result)).astype(brain_float_sixteen)
    return (mesh_state_gradient, d_grid, g_proc_qkv, g_proc_out, g_dec_q, g_dec_kv, g_dec_out)
```

```python
import jax
import jax.numpy as jnp
from jax import lax
from jax.experimental import pallas as pl
from jax.experimental.pallas import tpu as pltpu
from jax.sharding import PartitionSpec as P

HEAD_DIM = 64
EDGES = 4
WINDOW = 128


NZ, NX, NC = 8, 4, 2
EPS = 1e-05
NEG = -1e30


def extended(shard, sides, width):
    for axis, dim in sides:
        peers, length = (lax.axis_size(axis), shard.shape[dim])
        up = [(i, (i + 1) % peers) for i in range(peers - 1)]
        down = [(j, i) for i, j in up]
        last = lax.slice_in_dim(shard, length - width, length, axis=dim)
        leading = lax.slice_in_dim(shard, 0, width, axis=dim)
        before = lax.ppermute(last, axis, up)
        after = lax.ppermute(leading, axis, down)
        shard = jnp.concatenate([before, shard, after], axis=dim)
    return shard


def layer_norm_forward(values):
    values = values.astype(jnp.float32)
    centre = jnp.mean(values, axis=-1, keepdims=True)
    shifted = values - centre
    rstd = lax.rsqrt(jnp.mean(shifted * shifted, axis=-1, keepdims=True) + EPS)
    return (shifted * rstd, rstd)


def layer_norm_backward(normed, rstd, upstream):
    first = jnp.mean(upstream, axis=-1, keepdims=True)
    second = jnp.mean(upstream * normed, axis=-1, keepdims=True)
    return rstd * (upstream - first - normed * second)


def back_dot(left, weight):
    return lax.dot_general(
        left, weight, (((1,), (1,)), ((), ())), preferred_element_type=jnp.float32
    )


def outer_sum(left, right):
    return lax.dot_general(
        left, right, (((0,), (0,)), ((), ())), preferred_element_type=jnp.float32
    )


def window_probs(query_heads, key_heads, base_row, total_rows):
    row_count = query_heads.shape[0]
    scores = jnp.einsum(
        "qhd,khd->hqk", query_heads, key_heads, preferred_element_type=jnp.float32
    ) * HEAD_DIM ** (-0.5)
    query_pos = base_row + jnp.arange(row_count, dtype=jnp.int32)
    key_pos = base_row - row_count + jnp.arange(key_heads.shape[0], dtype=jnp.int32)
    distance = query_pos[:, None] - key_pos[None, :]
    valid_pair = (
        (jnp.abs(distance) <= WINDOW) & (key_pos[None, :] >= 0) & (key_pos[None, :] < total_rows)
    )
    scores = jnp.where(valid_pair[None], scores, NEG)
    return jax.nn.softmax(scores, axis=-1)


def edge_pass(query, keys, values, local, count, upstream):
    row_count = query.shape[0]
    head_count = query.shape[1] // HEAD_DIM
    factor = HEAD_DIM ** (-0.5)
    query_heads = query.astype(jnp.float32).reshape(row_count, head_count, HEAD_DIM)
    keys_at = [
        keys[local[:, j]].astype(jnp.float32).reshape(row_count, head_count, HEAD_DIM)
        for j in range(EDGES)
    ]
    values_at = [
        values[local[:, j]].astype(jnp.float32).reshape(row_count, head_count, HEAD_DIM)
        for j in range(EDGES)
    ]
    scores = jnp.stack([jnp.sum(query_heads * item, axis=-1) for item in keys_at], axis=-1) * factor
    valid_edge = (jnp.arange(EDGES, dtype=jnp.int32)[None, :] < count[:, None])[:, None, :]
    scores = jnp.where(valid_edge, scores, NEG)
    weights = jax.nn.softmax(scores, axis=-1)
    output = weights[..., 0:1] * values_at[0]
    for j in range(1, EDGES):
        output = output + weights[..., j : j + 1] * values_at[j]
    up_heads = upstream.reshape(row_count, head_count, HEAD_DIM)
    dweight = jnp.stack([jnp.sum(up_heads * item, axis=-1) for item in values_at], axis=-1)
    dscore = weights * (dweight - jnp.sum(weights * dweight, axis=-1, keepdims=True))
    dquery = dscore[..., 0:1] * keys_at[0]
    for j in range(1, EDGES):
        dquery = dquery + dscore[..., j : j + 1] * keys_at[j]
    dquery = dquery * factor
    key_terms = jnp.stack(
        [dscore[..., j : j + 1] * query_heads * factor for j in range(EDGES)], axis=0
    )
    value_terms = jnp.stack([weights[..., j : j + 1] * up_heads for j in range(EDGES)], axis=0)
    segment_ids = jnp.transpose(local).reshape(-1)
    dkeys = jax.ops.segment_sum(
        key_terms.reshape(EDGES * row_count, -1), segment_ids, num_segments=keys.shape[0]
    )
    dvalues = jax.ops.segment_sum(
        value_terms.reshape(EDGES * row_count, -1), segment_ids, num_segments=keys.shape[0]
    )
    return (output.reshape(row_count, -1), dquery.reshape(row_count, -1), dkeys, dvalues)


def band_reduce_kernel(g_hbm, out_ref, g, ra, hb, rb, hc, rc, in_sem, send, recv):
    band = lax.axis_index("band")
    core = lax.rem(band, NC)
    x = lax.rem(lax.div(band, NC), NX)
    z = lax.div(band, NC * NX)
    load = pltpu.make_async_copy(g_hbm, g, in_sem)
    load.start()

    def at(zz, xx, cc):
        return {"band": (zz * NX + xx) * NC + cc}

    pair = at(z, x, 1 - core)
    x_peers = [at(z, lax.rem(x + d, NX), core) for d in range(1, NX)]
    z_peers = [at(lax.rem(z + d, NZ), x, core) for d in range(1, NZ)]
    barrier = pltpu.get_barrier_semaphore()
    for peer in [pair] + x_peers + z_peers:
        pl.semaphore_signal(barrier, inc=1, device_id=peer, device_id_type=pl.DeviceIdType.MESH)
    pl.semaphore_wait(barrier, 1 + (NX - 1) + (NZ - 1))
    load.wait()

    def push(src, dst, slot, peer):
        copy = pltpu.make_async_remote_copy(
            src_ref=src, dst_ref=dst, send_sem=send.at[slot], recv_sem=recv.at[slot],
            device_id=peer, device_id_type=pl.DeviceIdType.MESH,
        )
        copy.start()
        return copy

    first = push(g.at[1 - core], ra, 0, pair)
    first.wait()

    def add_pair(i, carry):
        xx, zz = lax.div(i, NZ), lax.rem(i, NZ)
        hb[xx, zz] = (g[core, xx, zz].astype(jnp.float32) + ra[xx, zz].astype(jnp.float32)).astype(jnp.bfloat16)
        return carry

    lax.fori_loop(0, NX * NZ, add_pair, 0)
    copies = [push(hb.at[lax.rem(x + d, NX)], rb.at[d - 1], d, x_peers[d - 1]) for d in range(1, NX)]
    for copy in copies:
        copy.wait()

    def add_x(zz, carry):
        total = hb[x, zz].astype(jnp.float32)
        for d in range(NX - 1):
            total = total + rb[d, zz].astype(jnp.float32)
        hc[zz] = total.astype(jnp.bfloat16)
        return carry

    lax.fori_loop(0, NZ, add_x, 0)
    copies = [push(hc.at[lax.rem(z + d, NZ)], rc.at[d - 1], NX - 1 + d, z_peers[d - 1]) for d in range(1, NZ)]
    for copy in copies:
        copy.wait()
    total = hc[z].astype(jnp.float32)
    for d in range(NZ - 1):
        total = total + rc[d].astype(jnp.float32)
    out_ref[...] = total


def band_reduce(grads):
    count, rows, columns = grads.shape
    part = rows // (NZ * NX * NC)
    grads = grads.astype(jnp.bfloat16).reshape(count, NZ, NX, NC, part, columns)
    grads = jnp.transpose(grads, (3, 2, 1, 0, 4, 5)).reshape(NC, NX, NZ, count * part, columns)
    chunk = (count * part, columns)
    slots = 1 + (NX - 1) + (NZ - 1)
    out = pl.pallas_call(
        band_reduce_kernel,
        out_shape=jax.ShapeDtypeStruct(chunk, jnp.float32),
        in_specs=[pl.BlockSpec(memory_space=pl.ANY)],
        out_specs=pl.BlockSpec(memory_space=pltpu.VMEM),
        scratch_shapes=[
            pltpu.VMEM((NC, NX, NZ) + chunk, jnp.bfloat16),
            pltpu.VMEM((NX, NZ) + chunk, jnp.bfloat16),
            pltpu.VMEM((NX, NZ) + chunk, jnp.bfloat16),
            pltpu.VMEM((NX - 1, NZ) + chunk, jnp.bfloat16),
            pltpu.VMEM((NZ,) + chunk, jnp.bfloat16),
            pltpu.VMEM((NZ - 1,) + chunk, jnp.bfloat16),
            pltpu.SemaphoreType.DMA,
            pltpu.SemaphoreType.DMA((slots,)),
            pltpu.SemaphoreType.DMA((slots,)),
        ],
        compiler_params=pltpu.CompilerParams(
            collective_id=0, has_side_effects=True, vmem_limit_bytes=40 * 2**20
        ),
    )(grads)
    return out.reshape(count, part, columns)


def body(
    mesh_node_state,
    grid_state,
    d_out,
    neighbours,
    edge_count,
    w_proc_qkv,
    w_proc_out,
    w_dec_q,
    w_dec_kv,
    w_dec_out,
):
    brain_float_sixteen = jnp.bfloat16
    band_count = lax.axis_size("band")
    band_index = lax.axis_index("band")
    mesh_rows = mesh_node_state.shape[0]
    total_rows = mesh_rows * band_count
    base_row = band_index * mesh_rows
    local_width = w_proc_qkv.shape[2]
    head_count = local_width // HEAD_DIM
    factor = HEAD_DIM ** (-0.5)
    input_centred_scaled, inverse_deviation_input = layer_norm_forward(mesh_node_state)
    mesh_state_normalised = input_centred_scaled.astype(brain_float_sixteen)
    query_p = jnp.dot(
        mesh_state_normalised, w_proc_qkv[0], preferred_element_type=jnp.float32
    ).astype(brain_float_sixteen)
    key_p = jnp.dot(
        mesh_state_normalised, w_proc_qkv[1], preferred_element_type=jnp.float32
    ).astype(brain_float_sixteen)
    value_p = jnp.dot(
        mesh_state_normalised, w_proc_qkv[2], preferred_element_type=jnp.float32
    ).astype(brain_float_sixteen)
    window_kv = extended(jnp.stack([key_p, value_p]), (("band", 1),), mesh_rows)
    query_heads = query_p.reshape(mesh_rows, head_count, HEAD_DIM)
    key_heads = window_kv[0].reshape(3 * mesh_rows, head_count, HEAD_DIM)
    value_heads = window_kv[1].reshape(3 * mesh_rows, head_count, HEAD_DIM)
    probs = window_probs(query_heads, key_heads, base_row, total_rows)
    probs_b = probs.astype(brain_float_sixteen)
    attended = jnp.einsum("hqk,khd->qhd", probs_b, value_heads, preferred_element_type=jnp.float32)
    attended = attended.reshape(mesh_rows, local_width).astype(brain_float_sixteen)
    mixed = lax.psum(
        jnp.dot(attended, w_proc_out, preferred_element_type=jnp.float32).astype(jnp.bfloat16),
        "chan",
    ).astype(jnp.float32)
    state_out = (mesh_node_state.astype(jnp.float32) + mixed).astype(brain_float_sixteen)
    yhat, rstd_y = layer_norm_forward(state_out)
    state_normed = yhat.astype(brain_float_sixteen)
    key_d = jnp.dot(state_normed, w_dec_kv[0], preferred_element_type=jnp.float32).astype(
        brain_float_sixteen
    )
    value_d = jnp.dot(state_normed, w_dec_kv[1], preferred_element_type=jnp.float32).astype(
        brain_float_sixteen
    )
    decoder_kv = extended(jnp.stack([key_d, value_d]), (("band", 1),), mesh_rows)
    ghat, rstd_g = layer_norm_forward(grid_state)
    grid_normed = ghat.astype(brain_float_sixteen)
    query_d = jnp.dot(grid_normed, w_dec_q, preferred_element_type=jnp.float32).astype(
        brain_float_sixteen
    )
    upstream = back_dot(d_out, w_dec_out)
    local = neighbours - base_row + mesh_rows
    dec_out, dquery, dkey_ext_d, dvalue_ext_d = edge_pass(
        query_d, decoder_kv[0], decoder_kv[1], local, edge_count, upstream
    )
    dkv_dec_ext = jnp.stack([dkey_ext_d, dvalue_ext_d])
    dec_rims = jnp.concatenate(
        [dkv_dec_ext[:, :mesh_rows], dkv_dec_ext[:, mesh_rows + mesh_rows :]], axis=1
    )
    dec_returned = extended(dec_rims.astype(jnp.bfloat16), (("band", 1),), mesh_rows).astype(
        dec_rims.dtype
    )
    dkv_dec = dkv_dec_ext[:, mesh_rows : mesh_rows + mesh_rows]
    dkv_dec = dkv_dec.at[:, :mesh_rows].add(dec_returned[:, :mesh_rows])
    dkv_dec = dkv_dec.at[:, mesh_rows - mesh_rows :].add(dec_returned[:, 3 * mesh_rows :])
    dkv_dec = dkv_dec.astype(brain_float_sixteen)
    dec_out = dec_out.astype(brain_float_sixteen)
    dquery = dquery.astype(brain_float_sixteen)
    dkey_d = dkv_dec[0]
    dvalue_d = dkv_dec[1]
    grad_dec_out = outer_sum(d_out, dec_out)
    grad_dec_q = outer_sum(grid_normed, dquery)
    grad_dec_kv = jnp.stack([outer_sum(state_normed, dkey_d), outer_sum(state_normed, dvalue_d)])
    grid_part = back_dot(dquery, w_dec_q)
    state_part = back_dot(dkey_d, w_dec_kv[0]) + back_dot(dvalue_d, w_dec_kv[1])
    feature_count = grid_state.shape[1]
    share_width = feature_count // lax.axis_size("chan")
    share_start = lax.axis_index("chan") * share_width
    grid_total, state_total = (
        lax.psum(grid_part.astype(jnp.bfloat16), "chan").astype(jnp.float32),
        lax.psum(state_part.astype(jnp.bfloat16), "chan").astype(jnp.float32),
    )
    grid_grad = d_out.astype(jnp.float32) + layer_norm_backward(ghat, rstd_g, grid_total)
    d_grid = lax.dynamic_slice_in_dim(grid_grad, share_start, share_width, 1).astype(
        brain_float_sixteen
    )
    state_gradient_value = layer_norm_backward(yhat, rstd_y, state_total)
    state_grad_b = state_gradient_value.astype(brain_float_sixteen)
    grad_proc_out = outer_sum(state_grad_b, attended)
    dattended = back_dot(state_grad_b, w_proc_out).astype(brain_float_sixteen)
    grad_heads = dattended.reshape(mesh_rows, head_count, HEAD_DIM)
    dvalue_ext = jnp.einsum("hqk,qhd->khd", probs_b, grad_heads, preferred_element_type=jnp.float32)
    dprob = jnp.einsum("qhd,khd->hqk", grad_heads, value_heads, preferred_element_type=jnp.float32)
    centre = jnp.sum(probs * dprob, axis=-1, keepdims=True)
    dscore = (probs * (dprob - centre)).astype(brain_float_sixteen)
    dquery_p = (
        jnp.einsum("hqk,khd->qhd", dscore, key_heads, preferred_element_type=jnp.float32) * factor
    )
    dkey_ext = (
        jnp.einsum("hqk,qhd->khd", dscore, query_heads, preferred_element_type=jnp.float32) * factor
    )
    dkv_ext = jnp.stack([dkey_ext, dvalue_ext]).reshape(2, 3 * mesh_rows, local_width)
    rims = jnp.concatenate([dkv_ext[:, :mesh_rows], dkv_ext[:, 2 * mesh_rows :]], axis=1)
    returned = extended(rims.astype(jnp.bfloat16), (("band", 1),), mesh_rows).astype(rims.dtype)
    dkv_own = (
        dkv_ext[:, mesh_rows : 2 * mesh_rows]
        + returned[:, :mesh_rows]
        + returned[:, 3 * mesh_rows :]
    )
    dkv_own = dkv_own.astype(brain_float_sixteen)
    dquery_p = dquery_p.reshape(mesh_rows, local_width).astype(brain_float_sixteen)
    dkey_p = dkv_own[0]
    dvalue_p = dkv_own[1]
    mesh_part = (
        back_dot(dquery_p, w_proc_qkv[0])
        + back_dot(dkey_p, w_proc_qkv[1])
        + back_dot(dvalue_p, w_proc_qkv[2])
    )
    mesh_gradient_total = lax.psum(mesh_part.astype(jnp.bfloat16), "chan").astype(jnp.float32)
    mesh_state_gradient = (
        state_gradient_value
        + layer_norm_backward(input_centred_scaled, inverse_deviation_input, mesh_gradient_total)
    ).astype(brain_float_sixteen)
    grad_proc_qkv = jnp.stack(
        [
            outer_sum(mesh_state_normalised, dquery_p),
            outer_sum(mesh_state_normalised, dkey_p),
            outer_sum(mesh_state_normalised, dvalue_p),
        ]
    )
    summed = band_reduce(
        jnp.concatenate(
            [grad_proc_qkv, grad_proc_out[None], grad_dec_q[None], grad_dec_kv, grad_dec_out[None]]
        )
    )
    return (mesh_state_gradient, d_grid, summed[0:3], summed[3].T, summed[4], summed[5:7], summed[7].T)


def solution(mesh):
    placed = (
        P("band", None),
        P("band", None),
        P("band", None),
        P("band", None),
        P("band"),
        P(None, None, "chan"),
        P("chan", None),
        P(None, "chan"),
        P(None, None, "chan"),
        P("chan", None),
    )
    return jax.shard_map(
        body,
        mesh=mesh,
        in_specs=placed,
        out_specs=(
            P("band", None),
            P("band", "chan"),
            P(None, "band", "chan"),
            P("chan", "band"),
            P("band", "chan"),
            P(None, "band", "chan"),
            P("chan", "band"),
        ),
        check_vma=False,
    )
```

```python
import jax
import jax.numpy as jnp
from jax import lax
from jax.experimental import pallas as pl
from jax.experimental.pallas import tpu as pltpu
from jax.sharding import PartitionSpec as P

NZ, NX, NC, NY = 8, 4, 2, 4
BANDS = NZ * NX * NC
D = 1024
ROWS = 128
POINTS = 512
COLS = 256
HEADS = 4
HEAD_DIM = 64
EDGES = 4
RIM = 16
WINDOW = 128
SHARE = ROWS // NY
PART = D // BANDS
EPS = 1e-05
NEG = -1e30
FACTOR = HEAD_DIM**-0.5
F32 = jnp.float32
BF16 = jnp.bfloat16
MESH = pl.DeviceIdType.MESH
GROUPS = (4, 2, 2)
REMOTE = 96


def dot_nn(a, b):
    return lax.dot_general(a, b, (((1,), (0,)), ((), ())), preferred_element_type=F32)


def dot_nt(a, b):
    return lax.dot_general(a, b, (((1,), (1,)), ((), ())), preferred_element_type=F32)


def dot_tn(a, b):
    return lax.dot_general(a, b, (((0,), (0,)), ((), ())), preferred_element_type=F32)


def normalise(values):
    values = values.astype(F32)
    centre = jnp.mean(values, axis=-1, keepdims=True)
    shifted = values - centre
    rstd = lax.rsqrt(jnp.mean(shifted * shifted, axis=-1, keepdims=True) + EPS)
    return shifted * rstd, rstd


def normalise_back(normed, rstd, upstream):
    first = jnp.mean(upstream, axis=-1, keepdims=True)
    second = jnp.mean(upstream * normed, axis=-1, keepdims=True)
    return rstd * (upstream - first - normed * second)


def head_masks(dtype):
    lane = lax.broadcasted_iota(jnp.int32, (1, COLS), 1)
    return [((lane >= h * HEAD_DIM) & (lane < (h + 1) * HEAD_DIM)).astype(F32).astype(dtype) for h in range(HEADS)]


def kernel(
    mesh_hbm, grid_hbm, dout_hbm, near_hbm, count_hbm, wqkv_hbm, wpo_hbm, wdq_hbm, wdkv_hbm, wdo_hbm,
    out_mesh, out_grid, out_qkv, out_po, out_dq, out_dkv, out_do,
    mesh_v, grid_v, dout_v, near_v, count_v, wqkv, wpo, wdq, wdkv, wdo,
    xhat, mn, mn_t, sn_t, sg_t, kv, qp, kbd, vbd, pt, dpt, attended,
    part1, part1_in, sn, gn, gn_t, dout_t, grstd, qd, ud,
    own_kv, rim_in, kbd_c, vbd_c, kbd_r, vbd_r, cc, cr, s_c, s_r, dw_c, dw_r, w_c, w_r, ds_c, ds_r,
    rim_out, rim_back, dkv_own, dec, dq, gb, gb_in, gstat, gstat_in,
    part2, part2_in, sgrad, sg, ring_out, ring_in, dqkv, part3, part3_in, back,
    g1, g2, g3, ra1, ra2, ra3, hb1, hb2, hb3, rb1, rb2, rb3, hc1, hc2, hc3, rc1, rc2, rc3,
    load_sem, send_sem, recv_sem,
):
    band = lax.axis_index("band")
    y = lax.axis_index("chan")
    core = lax.rem(band, NC)
    x = lax.rem(lax.div(band, NC), NX)
    z = lax.div(band, NC * NX)

    def at(zz, xx, c):
        return {"band": (zz * NX + xx) * NC + c}

    pair = at(z, x, 1 - core)
    x_peers = [at(z, lax.rem(x + d, NX), core) for d in range(1, NX)]
    z_peers = [at(lax.rem(z + d, NZ), x, core) for d in range(1, NZ)]
    y_peers = [{"chan": lax.rem(y + d, NY)} for d in range(1, NY)]
    above = {"band": lax.rem(band + 1, BANDS)}
    below = {"band": lax.rem(band + BANDS - 1, BANDS)}

    barrier = pltpu.get_barrier_semaphore()
    peers = [pair, above, below] + x_peers + y_peers + z_peers
    for peer in peers:
        pl.semaphore_signal(barrier, inc=1, device_id=peer, device_id_type=MESH)

    loads = []
    for i, (src, dst) in enumerate((
        (mesh_hbm, mesh_v), (wqkv_hbm, wqkv), (grid_hbm, grid_v), (wdq_hbm, wdq), (dout_hbm, dout_v), (wdo_hbm, wdo),
        (near_hbm, near_v), (count_hbm, count_v), (wpo_hbm, wpo), (wdkv_hbm, wdkv),
    )):
        load = pltpu.make_async_copy(src, dst, load_sem.at[i])
        load.start()
        loads.append(load)
    l_mesh, l_qkv, l_grid, l_dq, l_dout, l_do, l_near, l_count, l_po, l_dkv = loads

    used = []

    def push(src, dst, peer):
        slot = len(used)
        copy = pltpu.make_async_remote_copy(
            src_ref=src, dst_ref=dst, send_sem=send_sem.at[slot], recv_sem=recv_sem.at[slot],
            device_id=peer, device_id_type=MESH,
        )
        copy.start()
        used.append(copy)
        return copy

    def arrive(copies):
        for copy in copies:
            copy.wait_recv()

    masks = head_masks(BF16)
    masks_f = head_masks(F32)

    def scatter_share(partial, landing):
        return [push(partial.at[lax.rem(y + d, NY)], landing.at[d - 1], y_peers[d - 1]) for d in range(1, NY)]

    def gather_share(blocks):
        return [push(blocks.at[y], blocks.at[y], y_peers[d - 1]) for d in range(1, NY)]

    def share_sum(partial, landing):
        total = partial[y].astype(F32)
        for d in range(NY - 1):
            total = total + landing[d].astype(F32)
        return total

    def store_grad(group, first, left_t, right):
        width = right.shape[1] // COLS

        def rows(zz, carry):
            lhs = left_t[pl.ds(pl.multiple_of(zz * ROWS, ROWS), ROWS), :]
            value = dot_nn(lhs, right).astype(BF16)
            for xx in range(NX):
                for c in range(NC):
                    lo = (xx * NC + c) * PART
                    for m in range(width):
                        group[c, xx, zz, (first + m) * PART : (first + m + 1) * PART, :] = value[
                            lo : lo + PART, m * COLS : (m + 1) * COLS
                        ]
            return carry

        lax.fori_loop(0, NZ, rows, 0)

    def send_pair(group, landing):
        return [push(group.at[1 - core], landing, pair)]

    def add_pair(group, landing, half):
        def step(i, carry):
            xx, zz = lax.div(i, NZ), lax.rem(i, NZ)
            half[xx, zz] = (group[core, xx, zz].astype(F32) + landing[xx, zz].astype(F32)).astype(BF16)
            return carry

        lax.fori_loop(0, NX * NZ, step, 0)

    def send_x(half, landing):
        return [push(half.at[lax.rem(x + d, NX)], landing.at[d - 1], x_peers[d - 1]) for d in range(1, NX)]

    def add_x(half, landing, eighth):
        def step(zz, carry):
            total = half[x, zz].astype(F32)
            for d in range(NX - 1):
                total = total + landing[d, zz].astype(F32)
            eighth[zz] = total.astype(BF16)
            return carry

        lax.fori_loop(0, NZ, step, 0)

    def send_z(eighth, landing):
        return [push(eighth.at[lax.rem(z + d, NZ)], landing.at[d - 1], z_peers[d - 1]) for d in range(1, NZ)]

    def total_z(eighth, landing):
        total = eighth[z].astype(F32)
        for d in range(NZ - 1):
            total = total + landing[d].astype(F32)
        return total

    l_mesh.wait()
    xh, rstd_x = normalise(mesh_v[...])
    xhat[...] = xh
    mn[...] = xh.astype(BF16)
    l_qkv.wait()
    kv[1, 0] = dot_nn(mn[...], wqkv[1]).astype(BF16)
    kv[1, 1] = dot_nn(mn[...], wqkv[2]).astype(BF16)
    pl.semaphore_wait(barrier, len(peers))
    kv_copies = [push(kv.at[1], kv.at[0], above), push(kv.at[1], kv.at[2], below)]
    qp[...] = dot_nn(mn[...], wqkv[0]).astype(BF16)

    l_grid.wait()

    def grid_rows(i, carry):
        rows = pl.ds(pl.multiple_of(i * 64, 64), 64)
        gh, rstd = normalise(grid_v[rows, :])
        gn[rows, :] = gh.astype(BF16)
        grstd[rows, :] = jnp.broadcast_to(rstd, (64, 128))
        return carry

    lax.fori_loop(0, POINTS // 64, grid_rows, 0)
    mn_t[...] = mn[...].T

    arrive(kv_copies)

    def stack_heads(block, h):
        kbd[h, block * ROWS : (block + 1) * ROWS, :] = kv[block, 0] * masks[h]
        vbd[h, block * ROWS : (block + 1) * ROWS, :] = kv[block, 1] * masks[h]

    for h in range(HEADS):
        for block in range(3):
            stack_heads(block, h)
    span = 3 * ROWS
    pt[...] = dot_nt(kbd[...].reshape(HEADS * span, COLS), qp[...]).reshape(HEADS, span, ROWS)
    key_row = lax.broadcasted_iota(jnp.int32, (span, ROWS), 0)
    query_row = lax.broadcasted_iota(jnp.int32, (span, ROWS), 1)
    position = band * ROWS - ROWS + key_row
    valid = (
        (key_row >= query_row) & (key_row <= query_row + 2 * WINDOW)
        & (position >= 0) & (position < BANDS * ROWS)
    )

    def window_softmax(h, carry):
        score = jnp.where(valid, pt[h] * FACTOR, NEG)
        weight = jnp.exp(score - jnp.max(score, axis=0, keepdims=True))
        pt[h] = weight / jnp.sum(weight, axis=0, keepdims=True)
        return carry

    lax.fori_loop(0, HEADS, window_softmax, 0)
    probs_b = pt[...].astype(BF16).reshape(HEADS * span, ROWS)
    attended[...] = dot_tn(probs_b, vbd[...].reshape(HEADS * span, COLS)).astype(BF16)
    l_po.wait()
    part1[...] = dot_nn(attended[...], wpo[...]).astype(BF16).reshape(NY, SHARE, D)
    copies = scatter_share(part1, part1_in)

    l_dq.wait()
    qd[...] = dot_nn(gn[...], wdq[...]).astype(BF16)
    l_near.wait()
    l_count.wait()
    local = near_v[...] - band * ROWS
    count = count_v[...]

    def multiplicity(first, rows):
        mesh_row = lax.broadcasted_iota(jnp.int32, (rows, POINTS), 0) + first
        total = jnp.zeros((rows, POINTS), F32)
        for e in range(EDGES):
            hit = (local[e : e + 1] == mesh_row) & (count > e)
            total = total + jnp.where(hit, 1.0, 0.0)
        return total

    cc[...] = multiplicity(0, ROWS)
    cr[:RIM] = multiplicity(-RIM, RIM)
    cr[RIM:] = multiplicity(ROWS, RIM)

    arrive(copies)
    own_rows = pl.ds(pl.multiple_of(y * SHARE, SHARE), SHARE)
    state = (mesh_v[own_rows, :].astype(F32) + share_sum(part1, part1_in)).astype(BF16)
    yhat, rstd_y = normalise(state)
    sn[y] = yhat.astype(BF16)
    copies = gather_share(sn)

    l_dout.wait()
    l_do.wait()
    ud[...] = dot_nt(dout_v[...], wdo[...]).astype(BF16)
    l_dkv.wait()
    arrive(copies)

    state_normed = sn[...].reshape(ROWS, D)
    own_kv[0] = dot_nn(state_normed, wdkv[0]).astype(BF16)
    own_kv[1] = dot_nn(state_normed, wdkv[1]).astype(BF16)
    rim_copies = [
        push(own_kv.at[:, pl.ds(ROWS - RIM, RIM), :], rim_in.at[0], above),
        push(own_kv.at[:, pl.ds(0, RIM), :], rim_in.at[1], below),
    ]
    for h in range(HEADS):
        kbd_c[h] = own_kv[0] * masks[h]
        vbd_c[h] = own_kv[1] * masks[h]
    s_c[...] = dot_nt(kbd_c[...].reshape(HEADS * ROWS, COLS), qd[...]).reshape(HEADS, ROWS, POINTS)
    dw_c[...] = dot_nt(vbd_c[...].reshape(HEADS * ROWS, COLS), ud[...]).reshape(HEADS, ROWS, POINTS)
    arrive(rim_copies)
    for h in range(HEADS):
        for side in range(2):
            kbd_r[h, side * RIM : (side + 1) * RIM, :] = rim_in[side, 0] * masks[h]
            vbd_r[h, side * RIM : (side + 1) * RIM, :] = rim_in[side, 1] * masks[h]
    s_r[...] = dot_nt(kbd_r[...].reshape(HEADS * 2 * RIM, COLS), qd[...]).reshape(HEADS, 2 * RIM, POINTS)
    dw_r[...] = dot_nt(vbd_r[...].reshape(HEADS * 2 * RIM, COLS), ud[...]).reshape(HEADS, 2 * RIM, POINTS)

    def edge_softmax(h, carry):
        for lo in range(0, POINTS, 128):
            at_c, at_r = cc[:, lo : lo + 128], cr[:, lo : lo + 128]
            score_c = jnp.where(at_c > 0, s_c[h, :, lo : lo + 128] * FACTOR, NEG)
            score_r = jnp.where(at_r > 0, s_r[h, :, lo : lo + 128] * FACTOR, NEG)
            top = jnp.maximum(jnp.max(score_c, axis=0, keepdims=True), jnp.max(score_r, axis=0, keepdims=True))
            e_c = at_c * jnp.exp(score_c - top)
            e_r = at_r * jnp.exp(score_r - top)
            scale = 1.0 / (jnp.sum(e_c, axis=0, keepdims=True) + jnp.sum(e_r, axis=0, keepdims=True))
            e_c = e_c * scale
            e_r = e_r * scale
            d_c = dw_c[h, :, lo : lo + 128]
            d_r = dw_r[h, :, lo : lo + 128]
            centre = jnp.sum(e_c * d_c, axis=0, keepdims=True) + jnp.sum(e_r * d_r, axis=0, keepdims=True)
            w_c[h, :, lo : lo + 128] = e_c.astype(BF16)
            w_r[h, :, lo : lo + 128] = e_r.astype(BF16)
            ds_c[h, :, lo : lo + 128] = (e_c * (d_c - centre) * FACTOR).astype(BF16)
            ds_r[h, :, lo : lo + 128] = (e_r * (d_r - centre) * FACTOR).astype(BF16)
        return carry

    lax.fori_loop(0, HEADS, edge_softmax, 0)

    def own_head(product, rows):
        blocks = product.reshape(HEADS, rows, COLS)
        total = lax.index_in_dim(blocks, 0, 0, keepdims=False) * masks_f[0]
        for h in range(1, HEADS):
            total = total + lax.index_in_dim(blocks, h, 0, keepdims=False) * masks_f[h]
        return total

    def flat(ref):
        return ref[...].reshape(ref.shape[0] * ref.shape[1], ref.shape[2])

    dkr = own_head(dot_nn(flat(ds_r), qd[...]), 2 * RIM).astype(BF16)
    dvr = own_head(dot_nn(flat(w_r), ud[...]), 2 * RIM).astype(BF16)
    for side in range(2):
        rim_out[side, 0] = dkr[side * RIM : (side + 1) * RIM]
        rim_out[side, 1] = dvr[side * RIM : (side + 1) * RIM]
    rim_copies = [push(rim_out.at[0], rim_back.at[0], below), push(rim_out.at[1], rim_back.at[1], above)]
    dk = own_head(dot_nn(flat(ds_c), qd[...]), ROWS)
    dv = own_head(dot_nn(flat(w_c), ud[...]), ROWS)
    arrive(rim_copies)

    def fold(middle, which):
        low = middle[:RIM] + rim_back[1, which].astype(F32)
        high = middle[ROWS - RIM :] + rim_back[0, which].astype(F32)
        return jnp.concatenate([low, middle[RIM : ROWS - RIM], high], axis=0).astype(BF16)

    dkv_own[:, :COLS] = fold(dk, 0)
    dkv_own[:, COLS:] = fold(dv, 1)
    part2[...] = (
        (dot_nt(dkv_own[:, :COLS], wdkv[0]) + dot_nt(dkv_own[:, COLS:], wdkv[1])).astype(BF16).reshape(NY, SHARE, D)
    )
    copies = scatter_share(part2, part2_in)

    dec[...] = (dot_tn(flat(w_c), flat(vbd_c)) + dot_tn(flat(w_r), flat(vbd_r))).astype(BF16)
    dq[...] = (dot_tn(flat(ds_c), flat(kbd_c)) + dot_tn(flat(ds_r), flat(kbd_r))).astype(BF16)

    arrive(copies)
    sgrad[...] = normalise_back(yhat, rstd_y, share_sum(part2, part2_in))
    sg[y] = sgrad[...].astype(BF16)
    copies = gather_share(sg)

    dout_t[...] = dout_v[...].T
    gn_t[...] = gn[...].T
    store_grad(g1, 0, gn_t, dq[...])
    store_grad(g1, 1, dout_t, dec[...])
    sn_t[...] = state_normed.T
    store_grad(g1, 2, sn_t, dkv_own[...])
    pair1 = send_pair(g1, ra1)

    arrive(copies)
    state_grad_b = sg[...].reshape(ROWS, D)
    da = dot_nt(state_grad_b, wpo[...]).astype(BF16)
    dpt[...] = dot_nt(vbd[...].reshape(HEADS * span, COLS), da).reshape(HEADS, span, ROWS)

    def window_back(h, carry):
        prob = pt[h]
        dprob = dpt[h]
        centre = jnp.sum(prob * dprob, axis=0, keepdims=True)
        dpt[h] = prob * (dprob - centre)
        return carry

    lax.fori_loop(0, HEADS, window_back, 0)
    dscore = dpt[...].astype(BF16).reshape(HEADS * span, ROWS)
    dk_ext = own_head(dot_nn(dscore, qp[...]), span) * FACTOR
    dv_ext = own_head(dot_nn(pt[...].astype(BF16).reshape(HEADS * span, ROWS), da), span)
    ring_out[0, 0] = dk_ext[:ROWS].astype(BF16)
    ring_out[0, 1] = dv_ext[:ROWS].astype(BF16)
    ring_out[1, 0] = dk_ext[2 * ROWS :].astype(BF16)
    ring_out[1, 1] = dv_ext[2 * ROWS :].astype(BF16)
    ring_copies = [push(ring_out.at[0], ring_in.at[0], below), push(ring_out.at[1], ring_in.at[1], above)]
    dqkv[:, :COLS] = (
        dot_tn(dscore, kbd[...].reshape(HEADS * span, COLS)) * FACTOR
    ).astype(BF16)

    arrive(pair1)
    add_pair(g1, ra1, hb1)
    x1 = send_x(hb1, rb1)

    store_grad(g2, 0, mn_t, dqkv[:, :COLS])
    sg_t[...] = state_grad_b.T
    store_grad(g2, 1, sg_t, attended[...])
    pair2 = send_pair(g2, ra2)

    arrive(ring_copies)
    for which, ext in ((0, dk_ext), (1, dv_ext)):
        total = ext[ROWS : 2 * ROWS] + ring_in[0, which].astype(F32) + ring_in[1, which].astype(F32)
        dqkv[:, (which + 1) * COLS : (which + 2) * COLS] = total.astype(BF16)
    part3[...] = (
        (
            dot_nt(dqkv[:, :COLS], wqkv[0])
            + dot_nt(dqkv[:, COLS : 2 * COLS], wqkv[1])
            + dot_nt(dqkv[:, 2 * COLS :], wqkv[2])
        ).astype(BF16).reshape(NY, SHARE, D)
    )
    copies = scatter_share(part3, part3_in)
    store_grad(g3, 0, mn_t, dqkv[:, COLS:])
    pair3 = send_pair(g3, ra3)

    arrive(pair2)
    add_pair(g2, ra2, hb2)
    x2 = send_x(hb2, rb2)

    arrive(copies)
    own_x = xhat[own_rows, :]
    centred, rstd_own = normalise(mesh_v[own_rows, :])
    result = sgrad[...] + normalise_back(own_x, rstd_own, share_sum(part3, part3_in))
    back[y] = result.astype(BF16)
    back_copies = gather_share(back)

    arrive(pair3)
    add_pair(g3, ra3, hb3)
    x3 = send_x(hb3, rb3)

    def grid_part(i, carry):
        rows = pl.ds(pl.multiple_of(i * 128, 128), 128)
        value = dot_nt(dq[rows, :], wdq[...])
        first = jnp.mean(value, axis=-1, keepdims=True)
        second = jnp.mean(value * gn[rows, :].astype(F32), axis=-1, keepdims=True)
        lane = lax.broadcasted_iota(jnp.int32, (128, 128), 1)
        both = jnp.where(lane == 0, first, jnp.where(lane == 1, second, 0.0)).T
        gstat[i] = both[:8]
        for q in range(NY):
            gb[q, rows, :] = value[:, q * COLS : (q + 1) * COLS].astype(BF16)
        return carry

    lax.fori_loop(0, POINTS // 128, grid_part, 0)
    grid_copies = []
    for d in range(1, NY):
        grid_copies.append(push(gb.at[lax.rem(y + d, NY)], gb_in.at[d - 1], y_peers[d - 1]))
        grid_copies.append(push(gstat, gstat_in.at[d - 1], y_peers[d - 1]))

    arrive(x1)
    add_x(hb1, rb1, hc1)
    z1 = send_z(hc1, rc1)
    arrive(x2)
    add_x(hb2, rb2, hc2)
    z2 = send_z(hc2, rc2)
    arrive(x3)
    add_x(hb3, rb3, hc3)
    z3 = send_z(hc3, rc3)

    arrive(grid_copies)
    columns = pl.ds(pl.multiple_of(y * COLS, COLS), COLS)

    def grid_final(i, carry):
        rows = pl.ds(pl.multiple_of(i * 128, 128), 128)
        stat = gstat[i]
        value = gb[y, rows, :].astype(F32)
        for d in range(NY - 1):
            stat = stat + gstat_in[d, i]
            value = value + gb_in[d, rows, :].astype(F32)
        stat = jnp.concatenate([stat, jnp.zeros((120, 128), F32)], axis=0).T
        change = value - stat[:, 0:1] - gn[rows, columns].astype(F32) * stat[:, 1:2]
        out_grid[rows, :] = (dout_v[rows, columns].astype(F32) + grstd[rows, 0:1] * change).astype(BF16)
        return carry

    lax.fori_loop(0, POINTS // 128, grid_final, 0)
    arrive(back_copies)
    out_mesh[...] = back[...].reshape(ROWS, D)

    arrive(z1)
    total = total_z(hc1, rc1)
    out_dq[...] = total[:PART]
    out_do[...] = total[PART : 2 * PART]
    out_dkv[0] = total[2 * PART : 3 * PART]
    out_dkv[1] = total[3 * PART :]
    arrive(z2)
    total = total_z(hc2, rc2)
    out_qkv[0] = total[:PART]
    out_po[...] = total[PART:]
    arrive(z3)
    total = total_z(hc3, rc3)
    out_qkv[1] = total[:PART]
    out_qkv[2] = total[PART:]
    for copy in used:
        copy.wait_send()


def body(
    mesh_node_state, grid_state, d_out, neighbours, edge_count, w_proc_qkv, w_proc_out, w_dec_q, w_dec_kv, w_dec_out
):
    span = 3 * ROWS
    v = pltpu.VMEM

    def reduce_scratch(make):
        return [make(n * PART) for n in GROUPS]

    scratch = [
        v((ROWS, D), BF16), v((POINTS, D), BF16), v((POINTS, D), BF16), v((EDGES, POINTS), jnp.int32),
        v((1, POINTS), jnp.int32), v((3, D, COLS), BF16), v((COLS, D), BF16), v((D, COLS), BF16),
        v((2, D, COLS), BF16), v((COLS, D), BF16),
        v((ROWS, D), F32), v((ROWS, D), BF16), v((D, ROWS), BF16), v((D, ROWS), BF16), v((D, ROWS), BF16), v((3, 2, ROWS, COLS), BF16), v((ROWS, COLS), BF16),
        v((HEADS, span, COLS), BF16), v((HEADS, span, COLS), BF16), v((HEADS, span, ROWS), F32),
        v((HEADS, span, ROWS), F32), v((ROWS, COLS), BF16),
        v((NY, SHARE, D), BF16), v((NY - 1, SHARE, D), BF16), v((NY, SHARE, D), BF16), v((POINTS, D), BF16),
        v((D, POINTS), BF16), v((D, POINTS), BF16), v((POINTS, 128), F32), v((POINTS, COLS), BF16),
        v((POINTS, COLS), BF16),
        v((2, ROWS, COLS), BF16), v((2, 2, RIM, COLS), BF16),
        v((HEADS, ROWS, COLS), BF16), v((HEADS, ROWS, COLS), BF16),
        v((HEADS, 2 * RIM, COLS), BF16), v((HEADS, 2 * RIM, COLS), BF16),
        v((ROWS, POINTS), F32), v((2 * RIM, POINTS), F32),
        v((HEADS, ROWS, POINTS), F32), v((HEADS, 2 * RIM, POINTS), F32),
        v((HEADS, ROWS, POINTS), F32), v((HEADS, 2 * RIM, POINTS), F32),
        v((HEADS, ROWS, POINTS), BF16), v((HEADS, 2 * RIM, POINTS), BF16),
        v((HEADS, ROWS, POINTS), BF16), v((HEADS, 2 * RIM, POINTS), BF16),
        v((2, 2, RIM, COLS), BF16), v((2, 2, RIM, COLS), BF16), v((ROWS, 2 * COLS), BF16),
        v((POINTS, COLS), BF16), v((POINTS, COLS), BF16), v((NY, POINTS, COLS), BF16),
        v((NY - 1, POINTS, COLS), BF16), v((POINTS // 128, 8, 128), F32), v((NY - 1, POINTS // 128, 8, 128), F32),
        v((NY, SHARE, D), BF16), v((NY - 1, SHARE, D), BF16), v((SHARE, D), F32), v((NY, SHARE, D), BF16),
        v((2, 2, ROWS, COLS), BF16), v((2, 2, ROWS, COLS), BF16), v((ROWS, 3 * COLS), BF16),
        v((NY, SHARE, D), BF16), v((NY - 1, SHARE, D), BF16), v((NY, SHARE, D), BF16),
    ]
    scratch += reduce_scratch(lambda r: v((NC, NX, NZ, r, COLS), BF16))
    scratch += reduce_scratch(lambda r: v((NX, NZ, r, COLS), BF16))
    scratch += reduce_scratch(lambda r: v((NX, NZ, r, COLS), BF16))
    scratch += reduce_scratch(lambda r: v((NX - 1, NZ, r, COLS), BF16))
    scratch += reduce_scratch(lambda r: v((NZ, r, COLS), BF16))
    scratch += reduce_scratch(lambda r: v((NZ - 1, r, COLS), BF16))
    scratch += [
        pltpu.SemaphoreType.DMA((10,)), pltpu.SemaphoreType.DMA((REMOTE,)), pltpu.SemaphoreType.DMA((REMOTE,)),
    ]
    shapes = (
        ((ROWS, D), BF16), ((POINTS, COLS), BF16), ((3, PART, COLS), F32), ((PART, COLS), F32),
        ((PART, COLS), F32), ((2, PART, COLS), F32), ((PART, COLS), F32),
    )
    mesh_grad, grid_grad, g_qkv, g_po, g_dq, g_dkv, g_do = pl.pallas_call(
        kernel,
        out_shape=[jax.ShapeDtypeStruct(shape, kind) for shape, kind in shapes],
        in_specs=[pl.BlockSpec(memory_space=pl.ANY)] * 10,
        out_specs=[pl.BlockSpec(memory_space=pltpu.VMEM)] * 7,
        scratch_shapes=scratch,
        compiler_params=pltpu.CompilerParams(
            collective_id=0, has_side_effects=True, vmem_limit_bytes=56 * 2**20
        ),
    )(
        mesh_node_state, grid_state, d_out, neighbours.T, edge_count.reshape(1, POINTS),
        w_proc_qkv, w_proc_out, w_dec_q, w_dec_kv, w_dec_out,
    )
    return mesh_grad, grid_grad, g_qkv, g_po.T, g_dq, g_dkv, g_do.T


def solution(mesh):
    placed = (
        P("band", None), P("band", None), P("band", None), P("band", None), P("band"),
        P(None, None, "chan"), P("chan", None), P(None, "chan"), P(None, None, "chan"), P("chan", None),
    )
    return jax.shard_map(
        body,
        mesh=mesh,
        in_specs=placed,
        out_specs=(
            P("band", None), P("band", "chan"), P(None, "band", "chan"), P("chan", "band"),
            P("band", "chan"), P(None, "band", "chan"), P("chan", "band"),
        ),
        check_vma=False,
    )
```

```python
import jax
import jax.numpy as jnp
from jax import lax
from jax.experimental import pallas as pl
from jax.experimental.pallas import tpu as pltpu
from jax.sharding import PartitionSpec as P

NZ, NX, NC, NY = 8, 4, 2, 4
BANDS = NZ * NX * NC
D = 1024
ROWS = 128
POINTS = 512
COLS = 256
HEADS = 4
HEAD_DIM = 64
EDGES = 4
RIM = 16
WINDOW = 128
SHARE = ROWS // NY
PART = D // BANDS
EPS = 1e-05
NEG = -1e30
FACTOR = HEAD_DIM**-0.5
F32 = jnp.float32
BF16 = jnp.bfloat16
MESH = pl.DeviceIdType.MESH
GROUPS = (2, 2, 2, 2)
HALF = NZ // 2
REMOTE = 112


def dot_nn(a, b):
    return lax.dot_general(a, b, (((1,), (0,)), ((), ())), preferred_element_type=F32)


def dot_nt(a, b):
    return lax.dot_general(a, b, (((1,), (1,)), ((), ())), preferred_element_type=F32)


def dot_tn(a, b):
    return lax.dot_general(a, b, (((0,), (0,)), ((), ())), preferred_element_type=F32)


def normalise(values):
    values = values.astype(F32)
    centre = jnp.mean(values, axis=-1, keepdims=True)
    shifted = values - centre
    rstd = lax.rsqrt(jnp.mean(shifted * shifted, axis=-1, keepdims=True) + EPS)
    return shifted * rstd, rstd


def normalise_back(normed, rstd, upstream):
    first = jnp.mean(upstream, axis=-1, keepdims=True)
    second = jnp.mean(upstream * normed, axis=-1, keepdims=True)
    return rstd * (upstream - first - normed * second)


def head_masks(dtype):
    lane = lax.broadcasted_iota(jnp.int32, (1, COLS), 1)
    return [((lane >= h * HEAD_DIM) & (lane < (h + 1) * HEAD_DIM)).astype(F32).astype(dtype) for h in range(HEADS)]


def kernel(
    mesh_hbm, grid_hbm, dout_hbm, near_hbm, count_hbm, wqkv_hbm, wpo_hbm, wdq_hbm, wdkv_hbm, wdo_hbm,
    out_mesh, out_grid, out_qkv, out_po, out_dq, out_dkv, out_do,
    mesh_v, grid_v, dout_v, near_v, count_v, wqkv, wpo, wdq, wdkv, wdo,
    xhat, mn, mn_t, mn_own_t, sn_t, sg_t, kv, qp, kbd, vbd, pt, dpt, attended,
    part1, part1_in, sn, gn, gn_t, dout_t, grstd, qd, ud,
    own_kv, kbd_c, vbd_c, kbd_r, vbd_r, cc, cr, s_c, s_r, dw_c, dw_r, w_c, w_r, ds_c, ds_r,
    dkv_ext, dec, dq, gb, gb_in, gstat, gstat_in,
    part2, part2_in, rim2_in, share, sgrad, sg, ring_out, ring_in, dkv3, dqkv, part3, part3_in, back,
    g0, g1, g2, g3, ra0, ra1, ra2, ra3, hb0, hb1, hb2, hb3, ry0, ry1, ry2, ry3,
    rb0, rb1, rb2, rb3, hc0, hc1, hc2, hc3, rc0, rc1, rc2, rc3,
    load_sem, send_sem, recv_sem, rim_send, rim_recv, rim2_send, rim2_recv,
):
    band = lax.axis_index("band")
    y = lax.axis_index("chan")
    core = lax.rem(band, NC)
    x = lax.rem(lax.div(band, NC), NX)
    z = lax.div(band, NC * NX)

    def at(zz, xx, c):
        return {"band": (zz * NX + xx) * NC + c}

    pair = at(z, x, 1 - core)
    x_peers = [at(z, lax.rem(x + d, NX), core) for d in (1, NX - 1)]
    z_peers = [at(lax.rem(z + d, NZ), x, core) for d in range(1, NZ)]
    y_peers = [{"chan": lax.rem(y + d, NY)} for d in range(1, NY)]
    above = {"band": lax.rem(band + 1, BANDS)}
    below = {"band": lax.rem(band + BANDS - 1, BANDS)}

    lower = [{"band": (band + BANDS - 1) % BANDS, "chan": c} for c in range(NY)]
    upper = [{"band": (band + 1) % BANDS, "chan": c} for c in range(NY)]

    barrier = pltpu.get_barrier_semaphore()

    def greet(peers):
        for peer in peers:
            pl.semaphore_signal(barrier, inc=1, device_id=peer, device_id_type=MESH)

    peers = [pair, above, below, lower[NY - 1], upper[0]] + x_peers + y_peers + z_peers
    greet(peers)

    @pl.when(y == 0)
    def _():
        greet(lower)

    @pl.when(y == NY - 1)
    def _():
        greet(upper)

    loads = []
    for i, (src, dst) in enumerate((
        (mesh_hbm, mesh_v), (wqkv_hbm, wqkv), (grid_hbm, grid_v), (wdq_hbm, wdq), (dout_hbm, dout_v), (wdo_hbm, wdo),
        (near_hbm, near_v), (count_hbm, count_v), (wpo_hbm, wpo), (wdkv_hbm, wdkv),
    )):
        load = pltpu.make_async_copy(src, dst, load_sem.at[i])
        load.start()
        loads.append(load)
    l_mesh, l_qkv, l_grid, l_dq, l_dout, l_do, l_near, l_count, l_po, l_dkv = loads

    used = []

    def push(src, dst, peer):
        slot = len(used)
        copy = pltpu.make_async_remote_copy(
            src_ref=src, dst_ref=dst, send_sem=send_sem.at[slot], recv_sem=recv_sem.at[slot],
            device_id=peer, device_id_type=MESH,
        )
        copy.start()
        used.append(copy)
        return copy

    def arrive(copies):
        for copy in copies:
            copy.wait_recv()

    masks = head_masks(BF16)
    masks_f = head_masks(F32)

    def scatter_share(partial, landing):
        return [push(partial.at[lax.rem(y + d, NY)], landing.at[d - 1], y_peers[d - 1]) for d in range(1, NY)]

    def gather_share(blocks):
        return [push(blocks.at[y], blocks.at[y], y_peers[d - 1]) for d in range(1, NY)]

    def share_sum(partial, landing):
        total = partial[y].astype(F32)
        for d in range(NY - 1):
            total = total + landing[d].astype(F32)
        return total

    def store_grad(group, first, left_t, right):
        width = right.shape[1] // COLS

        def rows(zz, carry):
            lhs = left_t[pl.ds(pl.multiple_of(zz * ROWS, ROWS), ROWS), :]
            value = dot_nn(lhs, right).astype(BF16)
            for xx in range(NX):
                for c in range(NC):
                    lo = (xx * NC + c) * PART
                    for m in range(width):
                        group[c, xx, zz, (first + m) * PART : (first + m + 1) * PART, :] = value[
                            lo : lo + PART, m * COLS : (m + 1) * COLS
                        ]
            return carry

        lax.fori_loop(0, NZ, rows, 0)

    def send_pair(group, landing):
        return [push(group.at[1 - core], landing, pair)]

    def add_pair(group, landing, half):
        def step(i, carry):
            xx, zz = lax.div(i, NZ), lax.rem(i, NZ)
            half[xx, zz] = (group[core, xx, zz].astype(F32) + landing[xx, zz].astype(F32)).astype(BF16)
            return carry

        lax.fori_loop(0, NX * NZ, step, 0)

    right_x, left_x = at(z, lax.rem(x + 1, NX), core), at(z, lax.rem(x + NX - 1, NX), core)
    to_right, to_left, across = lax.rem(x + 1, NX), lax.rem(x + NX - 1, NX), lax.rem(x + 2, NX)
    near, far = pl.ds(0, HALF), pl.ds(HALF, HALF)

    def send_x(half, relay, landing):
        first = [
            push(half.at[across, near], relay.at[0], right_x),
            push(half.at[across, far], relay.at[1], left_x),
        ]
        second = [
            push(half.at[to_right, far], landing.at[0, far], right_x),
            push(half.at[to_left, near], landing.at[1, near], left_x),
        ]
        return first, second

    def relay_x(first, second, half, relay, landing):
        arrive(first)

        def step(i, carry):
            half[to_right, i] = (half[to_right, i].astype(F32) + relay[0, i].astype(F32)).astype(BF16)
            half[to_left, HALF + i] = (half[to_left, HALF + i].astype(F32) + relay[1, i].astype(F32)).astype(BF16)
            return carry

        lax.fori_loop(0, HALF, step, 0)
        return second + [
            push(half.at[to_right, near], landing.at[0, near], right_x),
            push(half.at[to_left, far], landing.at[1, far], left_x),
        ]

    def add_x(half, landing, eighth):
        def step(zz, carry):
            total = half[x, zz].astype(F32) + landing[0, zz].astype(F32) + landing[1, zz].astype(F32)
            eighth[zz] = total.astype(BF16)
            return carry

        lax.fori_loop(0, NZ, step, 0)

    def send_z(eighth, landing):
        return [push(eighth.at[lax.rem(z + d, NZ)], landing.at[d - 1], z_peers[d - 1]) for d in range(1, NZ)]

    def total_z(eighth, landing):
        total = eighth[z].astype(F32)
        for d in range(NZ - 1):
            total = total + landing[d].astype(F32)
        return total

    l_mesh.wait()
    xh, rstd_x = normalise(mesh_v[...])
    xhat[...] = xh
    mn[1] = xh.astype(BF16)
    l_qkv.wait()
    kv[1, 0] = dot_nn(mn[1], wqkv[1]).astype(BF16)
    kv[1, 1] = dot_nn(mn[1], wqkv[2]).astype(BF16)
    outer = lax.div(y, NY - 1) + lax.div(NY - 1 - y, NY - 1)
    pl.semaphore_wait(barrier, len(peers) + NY * outer)
    kv_copies = [push(kv.at[1], kv.at[0], above), push(kv.at[1], kv.at[2], below)]
    mn_copies = [push(mn.at[1], mn.at[0], above), push(mn.at[1], mn.at[2], below)]
    qp[...] = dot_nn(mn[1], wqkv[0]).astype(BF16)

    l_grid.wait()

    def grid_rows(i, carry):
        rows = pl.ds(pl.multiple_of(i * 64, 64), 64)
        gh, rstd = normalise(grid_v[rows, :])
        gn[rows, :] = gh.astype(BF16)
        grstd[rows, :] = jnp.broadcast_to(rstd, (64, 128))
        return carry

    lax.fori_loop(0, POINTS // 64, grid_rows, 0)
    l_dq.wait()
    qd[...] = dot_nn(gn[...], wdq[...]).astype(BF16)
    gn_t[...] = gn[...].T

    arrive(kv_copies)

    def stack_heads(block, h):
        kbd[h, block * ROWS : (block + 1) * ROWS, :] = kv[block, 0] * masks[h]
        vbd[h, block * ROWS : (block + 1) * ROWS, :] = kv[block, 1] * masks[h]

    for h in range(HEADS):
        for block in range(3):
            stack_heads(block, h)
    span = 3 * ROWS
    pt[...] = dot_nt(kbd[...].reshape(HEADS * span, COLS), qp[...]).reshape(HEADS, span, ROWS)
    key_row = lax.broadcasted_iota(jnp.int32, (span, ROWS), 0)
    query_row = lax.broadcasted_iota(jnp.int32, (span, ROWS), 1)
    position = band * ROWS - ROWS + key_row
    valid = (
        (key_row >= query_row) & (key_row <= query_row + 2 * WINDOW)
        & (position >= 0) & (position < BANDS * ROWS)
    )

    def window_softmax(h, carry):
        score = jnp.where(valid, pt[h] * FACTOR, NEG)
        weight = jnp.exp(score - jnp.max(score, axis=0, keepdims=True))
        pt[h] = weight / jnp.sum(weight, axis=0, keepdims=True)
        return carry

    lax.fori_loop(0, HEADS, window_softmax, 0)
    probs_b = pt[...].astype(BF16).reshape(HEADS * span, ROWS)
    attended[...] = dot_tn(probs_b, vbd[...].reshape(HEADS * span, COLS)).astype(BF16)
    l_po.wait()
    part1[...] = dot_nn(attended[...], wpo[...]).astype(BF16).reshape(NY, SHARE, D)
    copies = scatter_share(part1, part1_in)

    l_dout.wait()
    l_do.wait()
    ud[...] = dot_nt(dout_v[...], wdo[...]).astype(BF16)
    dout_t[...] = dout_v[...].T
    l_near.wait()
    l_count.wait()
    local = near_v[...] - band * ROWS
    count = count_v[...]

    def multiplicity(first, rows):
        mesh_row = lax.broadcasted_iota(jnp.int32, (rows, POINTS), 0) + first
        total = jnp.zeros((rows, POINTS), F32)
        for e in range(EDGES):
            hit = (local[e : e + 1] == mesh_row) & (count > e)
            total = total + jnp.where(hit, 1.0, 0.0)
        return total

    cc[...] = multiplicity(0, ROWS)
    cr[:RIM] = multiplicity(-RIM, RIM)
    cr[RIM:] = multiplicity(ROWS, RIM)

    arrive(copies)
    own_rows = pl.ds(pl.multiple_of(y * SHARE, SHARE), SHARE)
    state = (mesh_v[own_rows, :].astype(F32) + share_sum(part1, part1_in)).astype(BF16)
    yhat, rstd_y = normalise(state)
    sn[y] = yhat.astype(BF16)
    copies = gather_share(sn)

    def rim_copy(c, side):
        row, dst = ((0, RIM), (SHARE - RIM, 0))[side]
        return pltpu.make_async_remote_copy(
            src_ref=sn.at[y, pl.ds(row, RIM), :], dst_ref=sn.at[NY, pl.ds(dst, RIM), :],
            send_sem=rim_send.at[c], recv_sem=rim_recv.at[side],
            device_id=(lower, upper)[side][c], device_id_type=MESH,
        )

    @pl.when(y == 0)
    def _():
        for c in range(NY):
            rim_copy(c, 0).start()

    @pl.when(y == NY - 1)
    def _():
        for c in range(NY):
            rim_copy(c, 1).start()

    arrive(mn_copies)
    mn_t[...] = mn[...].reshape(3 * ROWS, D).T
    l_dkv.wait()
    arrive(copies)
    rim_copy(0, 0).wait_recv()
    rim_copy(0, 1).wait_recv()

    state_normed = sn[...].reshape(ROWS + 2 * RIM, D)
    sn_t[...] = state_normed.T
    own_kv[0] = dot_nn(state_normed, wdkv[0]).astype(BF16)
    own_kv[1] = dot_nn(state_normed, wdkv[1]).astype(BF16)
    for h in range(HEADS):
        kbd_c[h] = own_kv[0, :ROWS, :] * masks[h]
        vbd_c[h] = own_kv[1, :ROWS, :] * masks[h]
        kbd_r[h] = own_kv[0, ROWS:, :] * masks[h]
        vbd_r[h] = own_kv[1, ROWS:, :] * masks[h]
    s_c[...] = dot_nt(kbd_c[...].reshape(HEADS * ROWS, COLS), qd[...]).reshape(HEADS, ROWS, POINTS)
    dw_c[...] = dot_nt(vbd_c[...].reshape(HEADS * ROWS, COLS), ud[...]).reshape(HEADS, ROWS, POINTS)
    s_r[...] = dot_nt(kbd_r[...].reshape(HEADS * 2 * RIM, COLS), qd[...]).reshape(HEADS, 2 * RIM, POINTS)
    dw_r[...] = dot_nt(vbd_r[...].reshape(HEADS * 2 * RIM, COLS), ud[...]).reshape(HEADS, 2 * RIM, POINTS)

    def edge_softmax(h, carry):
        for lo in range(0, POINTS, 128):
            at_c, at_r = cc[:, lo : lo + 128], cr[:, lo : lo + 128]
            score_c = jnp.where(at_c > 0, s_c[h, :, lo : lo + 128] * FACTOR, NEG)
            score_r = jnp.where(at_r > 0, s_r[h, :, lo : lo + 128] * FACTOR, NEG)
            top = jnp.maximum(jnp.max(score_c, axis=0, keepdims=True), jnp.max(score_r, axis=0, keepdims=True))
            e_c = at_c * jnp.exp(score_c - top)
            e_r = at_r * jnp.exp(score_r - top)
            scale = 1.0 / (jnp.sum(e_c, axis=0, keepdims=True) + jnp.sum(e_r, axis=0, keepdims=True))
            e_c = e_c * scale
            e_r = e_r * scale
            d_c = dw_c[h, :, lo : lo + 128]
            d_r = dw_r[h, :, lo : lo + 128]
            centre = jnp.sum(e_c * d_c, axis=0, keepdims=True) + jnp.sum(e_r * d_r, axis=0, keepdims=True)
            w_c[h, :, lo : lo + 128] = e_c.astype(BF16)
            w_r[h, :, lo : lo + 128] = e_r.astype(BF16)
            ds_c[h, :, lo : lo + 128] = (e_c * (d_c - centre) * FACTOR).astype(BF16)
            ds_r[h, :, lo : lo + 128] = (e_r * (d_r - centre) * FACTOR).astype(BF16)
        return carry

    lax.fori_loop(0, HEADS, edge_softmax, 0)

    def own_head(product, rows):
        blocks = product.reshape(HEADS, rows, COLS)
        total = lax.index_in_dim(blocks, 0, 0, keepdims=False) * masks_f[0]
        for h in range(1, HEADS):
            total = total + lax.index_in_dim(blocks, h, 0, keepdims=False) * masks_f[h]
        return total

    def flat(ref):
        return ref[...].reshape(ref.shape[0] * ref.shape[1], ref.shape[2])

    for which, (upstream_c, upstream_r, right) in enumerate(((ds_c, ds_r, qd), (w_c, w_r, ud))):
        cols = slice(which * COLS, (which + 1) * COLS)
        dkv_ext[:ROWS, cols] = own_head(dot_nn(flat(upstream_c), right[...]), ROWS).astype(BF16)
        dkv_ext[ROWS:, cols] = own_head(dot_nn(flat(upstream_r), right[...]), 2 * RIM).astype(BF16)
    part2[...] = (
        (dot_nt(dkv_ext[:, :COLS], wdkv[0]) + dot_nt(dkv_ext[:, COLS:], wdkv[1]))
        .astype(BF16).reshape(NY + 1, SHARE, D)
    )
    copies = scatter_share(part2, part2_in)

    def rim2_copy(side, slot):
        return pltpu.make_async_remote_copy(
            src_ref=part2.at[NY, pl.ds(side * RIM, RIM), :], dst_ref=rim2_in.at[slot],
            send_sem=rim2_send.at[side], recv_sem=rim2_recv.at[slot],
            device_id=(lower[NY - 1], upper[0])[side], device_id_type=MESH,
        )

    rim2_copy(0, y).start()
    rim2_copy(1, y).start()

    dec[...] = (dot_tn(flat(w_c), flat(vbd_c)) + dot_tn(flat(w_r), flat(vbd_r))).astype(BF16)
    dq[...] = (dot_tn(flat(ds_c), flat(kbd_c)) + dot_tn(flat(ds_r), flat(kbd_r))).astype(BF16)

    store_grad(g0, 0, gn_t, dq[...])
    store_grad(g0, 1, dout_t, dec[...])
    pair0 = send_pair(g0, ra0)
    store_grad(g1, 0, sn_t, dkv_ext[...])
    pair1 = send_pair(g1, ra1)
    arrive(pair0)
    add_pair(g0, ra0, hb0)
    x0 = send_x(hb0, ry0, rb0)

    arrive(copies)
    share[...] = share_sum(part2, part2_in)

    def rim_sum():
        for c in range(NY):
            rim2_copy(0, c).wait_recv()
        total = rim2_in[0].astype(F32)
        for c in range(1, NY):
            total = total + rim2_in[c].astype(F32)
        return total

    @pl.when(y == 0)
    def _():
        share[:RIM, :] = share[:RIM, :] + rim_sum()

    @pl.when(y == NY - 1)
    def _():
        share[SHARE - RIM :, :] = share[SHARE - RIM :, :] + rim_sum()

    sgrad[...] = normalise_back(yhat, rstd_y, share[...])
    sg[y] = sgrad[...].astype(BF16)
    copies = gather_share(sg)

    def grid_part(i, carry):
        rows = pl.ds(pl.multiple_of(i * 128, 128), 128)
        half_rows = pl.ds(pl.multiple_of(lax.rem(i, 2) * 128, 128), 128)
        half = lax.div(i, 2)
        value = dot_nt(dq[rows, :], wdq[...])
        first = jnp.mean(value, axis=-1, keepdims=True)
        second = jnp.mean(value * gn[rows, :].astype(F32), axis=-1, keepdims=True)
        lane = lax.broadcasted_iota(jnp.int32, (128, 128), 1)
        both = jnp.where(lane == 0, first, jnp.where(lane == 1, second, 0.0)).T
        gstat[i] = both[:8]
        for q in range(NY):
            gb[half, q, half_rows, :] = value[:, q * COLS : (q + 1) * COLS].astype(BF16)
        return carry

    lax.fori_loop(0, POINTS // 128, grid_part, 0)

    def send_grid(half):
        return [
            push(gb.at[half, lax.rem(y + d, NY)], gb_in.at[half, d - 1], y_peers[d - 1]) for d in range(1, NY)
        ]

    arrive(pair1)
    add_pair(g1, ra1, hb1)
    x1 = send_x(hb1, ry1, rb1)
    x0 = relay_x(*x0, hb0, ry0, rb0)

    arrive(copies)
    grid_copies = send_grid(0)
    x1 = relay_x(*x1, hb1, ry1, rb1)
    state_grad_b = sg[...].reshape(ROWS, D)
    da = dot_nt(state_grad_b, wpo[...]).astype(BF16)
    dpt[...] = dot_nt(vbd[...].reshape(HEADS * span, COLS), da).reshape(HEADS, span, ROWS)

    def window_back(h, carry):
        prob = pt[h]
        dprob = dpt[h]
        centre = jnp.sum(prob * dprob, axis=0, keepdims=True)
        dpt[h] = prob * (dprob - centre)
        return carry

    lax.fori_loop(0, HEADS, window_back, 0)
    dscore = dpt[...].astype(BF16).reshape(HEADS * span, ROWS)
    dk_ext = own_head(dot_nn(dscore, qp[...]), span) * FACTOR
    dv_ext = own_head(dot_nn(pt[...].astype(BF16).reshape(HEADS * span, ROWS), da), span)
    for which, ext in ((0, dk_ext), (1, dv_ext)):
        rounded = ext.astype(BF16)
        dkv3[:, which * COLS : (which + 1) * COLS] = rounded
        ring_out[0, which] = rounded[:ROWS]
        ring_out[1, which] = rounded[2 * ROWS :]
    ring_copies = [push(ring_out.at[0], ring_in.at[0], below), push(ring_out.at[1], ring_in.at[1], above)]
    store_grad(g2, 0, mn_t, dkv3[...])
    pair2 = send_pair(g2, ra2)
    dqkv[:, :COLS] = (
        dot_tn(dscore, kbd[...].reshape(HEADS * span, COLS)) * FACTOR
    ).astype(BF16)
    mn_own_t[...] = mn_t[:, ROWS : 2 * ROWS]
    store_grad(g3, 0, mn_own_t, dqkv[:, :COLS])
    sg_t[...] = state_grad_b.T
    store_grad(g3, 1, sg_t, attended[...])
    pair3 = send_pair(g3, ra3)

    arrive(pair2)
    add_pair(g2, ra2, hb2)
    x2 = send_x(hb2, ry2, rb2)
    arrive(x0)
    add_x(hb0, rb0, hc0)
    z0 = send_z(hc0, rc0)

    arrive(ring_copies)
    for which, ext in ((0, dk_ext), (1, dv_ext)):
        total = ext[ROWS : 2 * ROWS] + ring_in[0, which].astype(F32) + ring_in[1, which].astype(F32)
        dqkv[:, (which + 1) * COLS : (which + 2) * COLS] = total.astype(BF16)
    part3[...] = (
        (
            dot_nt(dqkv[:, :COLS], wqkv[0])
            + dot_nt(dqkv[:, COLS : 2 * COLS], wqkv[1])
            + dot_nt(dqkv[:, 2 * COLS :], wqkv[2])
        ).astype(BF16).reshape(NY, SHARE, D)
    )
    copies = scatter_share(part3, part3_in)

    arrive(pair3)
    add_pair(g3, ra3, hb3)
    x3 = send_x(hb3, ry3, rb3)
    x2 = relay_x(*x2, hb2, ry2, rb2)

    arrive(x1)
    add_x(hb1, rb1, hc1)
    z1 = send_z(hc1, rc1)
    x3 = relay_x(*x3, hb3, ry3, rb3)

    arrive(copies)
    own_x = xhat[own_rows, :]
    centred, rstd_own = normalise(mesh_v[own_rows, :])
    result = sgrad[...] + normalise_back(own_x, rstd_own, share_sum(part3, part3_in))
    back[y] = result.astype(BF16)
    back_copies = gather_share(back)
    grid_copies += send_grid(1)
    for d in range(1, NY):
        grid_copies.append(push(gstat, gstat_in.at[d - 1], y_peers[d - 1]))

    arrive(x2)
    add_x(hb2, rb2, hc2)
    z2 = send_z(hc2, rc2)
    arrive(x3)
    add_x(hb3, rb3, hc3)
    z3 = send_z(hc3, rc3)

    arrive(grid_copies)
    columns = pl.ds(pl.multiple_of(y * COLS, COLS), COLS)

    def grid_final(i, carry):
        rows = pl.ds(pl.multiple_of(i * 128, 128), 128)
        stat = gstat[i]
        half_rows = pl.ds(pl.multiple_of(lax.rem(i, 2) * 128, 128), 128)
        half = lax.div(i, 2)
        value = gb[half, y, half_rows, :].astype(F32)
        for d in range(NY - 1):
            stat = stat + gstat_in[d, i]
            value = value + gb_in[half, d, half_rows, :].astype(F32)
        stat = jnp.concatenate([stat, jnp.zeros((120, 128), F32)], axis=0).T
        change = value - stat[:, 0:1] - gn[rows, columns].astype(F32) * stat[:, 1:2]
        out_grid[rows, :] = (dout_v[rows, columns].astype(F32) + grstd[rows, 0:1] * change).astype(BF16)
        return carry

    lax.fori_loop(0, POINTS // 128, grid_final, 0)
    arrive(back_copies)
    out_mesh[...] = back[...].reshape(ROWS, D)

    arrive(z0)
    total = total_z(hc0, rc0)
    out_dq[...] = total[:PART]
    out_do[...] = total[PART:]
    arrive(z1)
    total = total_z(hc1, rc1)
    out_dkv[0] = total[:PART]
    out_dkv[1] = total[PART:]
    arrive(z2)
    total = total_z(hc2, rc2)
    out_qkv[1] = total[:PART]
    out_qkv[2] = total[PART:]
    arrive(z3)
    total = total_z(hc3, rc3)
    out_qkv[0] = total[:PART]
    out_po[...] = total[PART:]
    rim2_copy(0, 0).wait_send()
    rim2_copy(1, 0).wait_send()

    @pl.when((y == 0) | (y == NY - 1))
    def _():
        for c in range(NY):
            rim_copy(c, 0).wait_send()

    for copy in used:
        copy.wait_send()


def copy_out(*refs):
    count = len(refs) // 2
    for source, target in zip(refs[:count], refs[count:]):
        target[...] = source[...]


def body(
    mesh_node_state, grid_state, d_out, neighbours, edge_count, w_proc_qkv, w_proc_out, w_dec_q, w_dec_kv, w_dec_out
):
    span = 3 * ROWS
    v = pltpu.VMEM

    def reduce_scratch(make):
        return [make(n * PART) for n in GROUPS]

    scratch = [
        v((ROWS, D), BF16), v((POINTS, D), BF16), v((POINTS, D), BF16), v((EDGES, POINTS), jnp.int32),
        v((1, POINTS), jnp.int32), v((3, D, COLS), BF16), v((COLS, D), BF16), v((D, COLS), BF16),
        v((2, D, COLS), BF16), v((COLS, D), BF16),
        v((ROWS, D), F32), v((3, ROWS, D), BF16), v((D, span), BF16), v((D, ROWS), BF16), v((D, ROWS + 2 * RIM), BF16), v((D, ROWS), BF16), v((3, 2, ROWS, COLS), BF16), v((ROWS, COLS), BF16),
        v((HEADS, span, COLS), BF16), v((HEADS, span, COLS), BF16), v((HEADS, span, ROWS), F32),
        v((HEADS, span, ROWS), F32), v((ROWS, COLS), BF16),
        v((NY, SHARE, D), BF16), v((NY - 1, SHARE, D), BF16), v((NY + 1, SHARE, D), BF16), v((POINTS, D), BF16),
        v((D, POINTS), BF16), v((D, POINTS), BF16), v((POINTS, 128), F32), v((POINTS, COLS), BF16),
        v((POINTS, COLS), BF16),
        v((2, ROWS + 2 * RIM, COLS), BF16),
        v((HEADS, ROWS, COLS), BF16), v((HEADS, ROWS, COLS), BF16),
        v((HEADS, 2 * RIM, COLS), BF16), v((HEADS, 2 * RIM, COLS), BF16),
        v((ROWS, POINTS), F32), v((2 * RIM, POINTS), F32),
        v((HEADS, ROWS, POINTS), F32), v((HEADS, 2 * RIM, POINTS), F32),
        v((HEADS, ROWS, POINTS), F32), v((HEADS, 2 * RIM, POINTS), F32),
        v((HEADS, ROWS, POINTS), BF16), v((HEADS, 2 * RIM, POINTS), BF16),
        v((HEADS, ROWS, POINTS), BF16), v((HEADS, 2 * RIM, POINTS), BF16),
        v((ROWS + 2 * RIM, 2 * COLS), BF16),
        v((POINTS, COLS), BF16), v((POINTS, COLS), BF16), v((2, NY, POINTS // 2, COLS), BF16),
        v((2, NY - 1, POINTS // 2, COLS), BF16), v((POINTS // 128, 8, 128), F32), v((NY - 1, POINTS // 128, 8, 128), F32),
        v((NY + 1, SHARE, D), BF16), v((NY - 1, SHARE, D), BF16), v((NY, RIM, D), BF16), v((SHARE, D), F32),
        v((SHARE, D), F32), v((NY, SHARE, D), BF16),
        v((2, 2, ROWS, COLS), BF16), v((2, 2, ROWS, COLS), BF16),
        v((span, 2 * COLS), BF16), v((ROWS, 3 * COLS), BF16),
        v((NY, SHARE, D), BF16), v((NY - 1, SHARE, D), BF16), v((NY, SHARE, D), BF16),
    ]
    scratch += reduce_scratch(lambda r: v((NC, NX, NZ, r, COLS), BF16))
    scratch += reduce_scratch(lambda r: v((NX, NZ, r, COLS), BF16))
    scratch += reduce_scratch(lambda r: v((NX, NZ, r, COLS), BF16))
    scratch += reduce_scratch(lambda r: v((2, HALF, r, COLS), BF16))
    scratch += reduce_scratch(lambda r: v((2, NZ, r, COLS), BF16))
    scratch += reduce_scratch(lambda r: v((NZ, r, COLS), BF16))
    scratch += reduce_scratch(lambda r: v((NZ - 1, r, COLS), BF16))
    scratch += [
        pltpu.SemaphoreType.DMA((10,)), pltpu.SemaphoreType.DMA((REMOTE,)), pltpu.SemaphoreType.DMA((REMOTE,)),
        pltpu.SemaphoreType.DMA((NY,)), pltpu.SemaphoreType.DMA((2,)), pltpu.SemaphoreType.DMA((2,)),
        pltpu.SemaphoreType.DMA((NY,)),
    ]
    shapes = (
        ((ROWS, D), BF16), ((POINTS, COLS), BF16), ((3, PART, COLS), F32), ((PART, COLS), F32),
        ((PART, COLS), F32), ((2, PART, COLS), F32), ((PART, COLS), F32),
    )
    results = pl.pallas_call(
        kernel,
        out_shape=[jax.ShapeDtypeStruct(shape, kind) for shape, kind in shapes],
        in_specs=[pl.BlockSpec(memory_space=pl.ANY)] * 10,
        out_specs=[pl.BlockSpec(memory_space=pltpu.VMEM)] * 7,
        scratch_shapes=scratch,
        compiler_params=pltpu.CompilerParams(
            collective_id=0, has_side_effects=True, vmem_limit_bytes=56 * 2**20
        ),
    )(
        mesh_node_state, grid_state, d_out, neighbours.T, edge_count.reshape(1, POINTS),
        w_proc_qkv, w_proc_out, w_dec_q, w_dec_kv, w_dec_out,
    )
    mesh_grad, grid_grad, g_qkv, g_po, g_dq, g_dkv, g_do = pl.pallas_call(
        copy_out,
        out_shape=[jax.ShapeDtypeStruct(shape, kind) for shape, kind in shapes],
        in_specs=[pl.BlockSpec(memory_space=pltpu.VMEM)] * 7,
        out_specs=[pl.BlockSpec(memory_space=pltpu.VMEM)] * 7,
    )(*results)
    return mesh_grad, grid_grad, g_qkv, g_po.T, g_dq, g_dkv, g_do.T


def solution(mesh):
    placed = (
        P("band", None), P("band", None), P("band", None), P("band", None), P("band"),
        P(None, None, "chan"), P("chan", None), P(None, "chan"), P(None, None, "chan"), P("chan", None),
    )
    return jax.shard_map(
        body,
        mesh=mesh,
        in_specs=placed,
        out_specs=(
            P("band", None), P("band", "chan"), P(None, "band", "chan"), P("chan", "band"),
            P("band", "chan"), P(None, "band", "chan"), P("chan", "band"),
        ),
        check_vma=False,
    )
```

```python
import jax
import jax.numpy as jnp
from jax import lax
from jax.experimental import pallas as pl
from jax.experimental.pallas import tpu as pltpu
from jax.sharding import PartitionSpec as P

NZ, NX, NC, NY = 8, 4, 2, 4
BANDS = NZ * NX * NC
D = 1024
ROWS = 128
POINTS = 512
COLS = 256
HEADS = 4
HEAD_DIM = 64
EDGES = 4
RIM = 16
WINDOW = 128
SHARE = ROWS // NY
PART = D // BANDS
EPS = 1e-05
NEG = -1e30
FACTOR = HEAD_DIM**-0.5
F32 = jnp.float32
BF16 = jnp.bfloat16
MESH = pl.DeviceIdType.MESH
GROUPS = (1, 2, 2, 1)
HALF = NZ // 2
REMOTE = 128


def dot_nn(a, b):
    return lax.dot_general(a, b, (((1,), (0,)), ((), ())), preferred_element_type=F32)


def dot_nt(a, b):
    return lax.dot_general(a, b, (((1,), (1,)), ((), ())), preferred_element_type=F32)


def dot_tn(a, b):
    return lax.dot_general(a, b, (((0,), (0,)), ((), ())), preferred_element_type=F32)


def normalise(values):
    values = values.astype(F32)
    centre = jnp.mean(values, axis=-1, keepdims=True)
    shifted = values - centre
    rstd = lax.rsqrt(jnp.mean(shifted * shifted, axis=-1, keepdims=True) + EPS)
    return shifted * rstd, rstd


def normalise_back(normed, rstd, upstream):
    first = jnp.mean(upstream, axis=-1, keepdims=True)
    second = jnp.mean(upstream * normed, axis=-1, keepdims=True)
    return rstd * (upstream - first - normed * second)


def head_masks(dtype):
    lane = lax.broadcasted_iota(jnp.int32, (1, COLS), 1)
    return [((lane >= h * HEAD_DIM) & (lane < (h + 1) * HEAD_DIM)).astype(F32).astype(dtype) for h in range(HEADS)]


def kernel(
    mesh_hbm, grid_hbm, dout_hbm, near_hbm, count_hbm, wqkv_hbm, wpo_hbm, wdq_hbm, wdkv_hbm, wdo_hbm,
    out_mesh, out_grid, out_qkv, out_po, out_dq, out_dkv, out_do,
    mesh_v, grid_v, dout_v, near_v, count_v, wqkv, wpo, wdq, wdkv, wdo,
    xhat, mn, mn_t, mn_own_t, sn_t, sg_t, kv, qp, kbd, vbd, pt, dpt, attended,
    part1, part1_in, sn, gn, gn_t, dout_t, grstd, qd, ud,
    own_kv, kbd_c, vbd_c, kbd_r, vbd_r, cc, cr, s_c, s_r, dw_c, dw_r, w_c, w_r, ds_c, ds_r,
    dkv_ext, dec, dq, gb, gb_in, gstat, gstat_in,
    part2, part2_in, rim2_in, share, sgrad, sg, ring_out, ring_in, dkv3, dqkv, part3, part3_in, back,
    g0, g1, g2, g3, ra0, ra1, ra2, ra3, hb0, hb1, hb2, hb3, ry0, ry1, ry2, ry3,
    rb0, rb1, rb2, rb3, hc0, hc1, hc2, hc3, rc0, rc1, rc2, rc3,
    ga, gq, raa, raq, hba, hbq, rza, rzq, hca, hcq, rxa, rxq,
    load_sem, send_sem, recv_sem, rim_send, rim_recv, rim2_send, rim2_recv,
):
    band = lax.axis_index("band")
    y = lax.axis_index("chan")
    core = lax.rem(band, NC)
    x = lax.rem(lax.div(band, NC), NX)
    z = lax.div(band, NC * NX)

    def at(zz, xx, c):
        return {"band": (zz * NX + xx) * NC + c}

    pair = at(z, x, 1 - core)
    x_peers = [at(z, lax.rem(x + d, NX), core) for d in range(1, NX)]
    across_x = x_peers[1]
    z_peers = [at(lax.rem(z + d, NZ), x, core) for d in range(1, NZ)]
    y_peers = [{"chan": lax.rem(y + d, NY)} for d in range(1, NY)]
    above = {"band": lax.rem(band + 1, BANDS)}
    below = {"band": lax.rem(band + BANDS - 1, BANDS)}

    lower = [{"band": (band + BANDS - 1) % BANDS, "chan": c} for c in range(NY)]
    upper = [{"band": (band + 1) % BANDS, "chan": c} for c in range(NY)]

    barrier = pltpu.get_barrier_semaphore()

    def greet(peers):
        for peer in peers:
            pl.semaphore_signal(barrier, inc=1, device_id=peer, device_id_type=MESH)

    peers = [pair, above, below, lower[NY - 1], upper[0]] + x_peers + y_peers + z_peers
    greet(peers)

    @pl.when(y == 0)
    def _():
        greet(lower)

    @pl.when(y == NY - 1)
    def _():
        greet(upper)

    loads = []
    for i, (src, dst) in enumerate((
        (mesh_hbm, mesh_v), (wqkv_hbm, wqkv), (grid_hbm, grid_v), (wdq_hbm, wdq), (dout_hbm, dout_v), (wdo_hbm, wdo),
        (near_hbm, near_v), (count_hbm, count_v), (wpo_hbm, wpo), (wdkv_hbm, wdkv),
    )):
        load = pltpu.make_async_copy(src, dst, load_sem.at[i])
        load.start()
        loads.append(load)
    l_mesh, l_qkv, l_grid, l_dq, l_dout, l_do, l_near, l_count, l_po, l_dkv = loads

    used = []

    def push(src, dst, peer):
        slot = len(used)
        copy = pltpu.make_async_remote_copy(
            src_ref=src, dst_ref=dst, send_sem=send_sem.at[slot], recv_sem=recv_sem.at[slot],
            device_id=peer, device_id_type=MESH,
        )
        copy.start()
        used.append(copy)
        return copy

    def arrive(copies):
        for copy in copies:
            copy.wait_recv()

    masks = head_masks(BF16)
    masks_f = head_masks(F32)

    def scatter_share(partial, landing):
        return [push(partial.at[lax.rem(y + d, NY)], landing.at[d - 1], y_peers[d - 1]) for d in range(1, NY)]

    def gather_share(blocks):
        return [push(blocks.at[y], blocks.at[y], y_peers[d - 1]) for d in range(1, NY)]

    def share_sum(partial, landing):
        total = partial[y].astype(F32)
        for d in range(NY - 1):
            total = total + landing[d].astype(F32)
        return total

    def store_grad(group, first, left_t, right):
        width = right.shape[1] // COLS

        def rows(zz, carry):
            lhs = left_t[pl.ds(pl.multiple_of(zz * ROWS, ROWS), ROWS), :]
            value = dot_nn(lhs, right).astype(BF16)
            for xx in range(NX):
                for c in range(NC):
                    lo = (xx * NC + c) * PART
                    for m in range(width):
                        group[c, xx, zz, (first + m) * PART : (first + m + 1) * PART, :] = value[
                            lo : lo + PART, m * COLS : (m + 1) * COLS
                        ]
            return carry

        lax.fori_loop(0, NZ, rows, 0)

    def send_pair(group, landing):
        return [push(group.at[1 - core], landing, pair)]

    def add_pair(group, landing, half):
        def step(xx, carry):
            for zz in range(NZ):
                half[xx, zz] = group[core, xx, zz] + landing[xx, zz]
            return carry

        lax.fori_loop(0, NX, step, 0)

    def add_pair_z(group, landing, half):
        def step(xx, carry):
            for zz in range(NZ):
                half[zz, xx] = group[core, xx, zz] + landing[xx, zz]
            return carry

        lax.fori_loop(0, NX, step, 0)

    def add_z(half, landing, eighth):
        for xx in range(NX):
            total = half[z, xx].astype(F32)
            for d in range(NZ - 1):
                total = total + landing[d, xx].astype(F32)
            eighth[xx] = total.astype(BF16)

    def send_x_last(eighth, landing):
        return [push(eighth.at[lax.rem(x + d, NX)], landing.at[d - 1], x_peers[d - 1]) for d in range(1, NX)]

    def total_x(eighth, landing):
        total = eighth[x].astype(F32)
        for d in range(NX - 1):
            total = total + landing[d].astype(F32)
        return total

    right_x, left_x = at(z, lax.rem(x + 1, NX), core), at(z, lax.rem(x + NX - 1, NX), core)
    to_right, to_left, across = lax.rem(x + 1, NX), lax.rem(x + NX - 1, NX), lax.rem(x + 2, NX)
    near, far = pl.ds(0, HALF), pl.ds(HALF, HALF)

    def send_x(half, relay, landing):
        first = [
            push(half.at[across, near], relay.at[0], right_x),
            push(half.at[across, far], relay.at[1], left_x),
        ]
        second = [
            push(half.at[to_right, far], landing.at[0, far], right_x),
            push(half.at[to_left, near], landing.at[1, near], left_x),
        ]
        return first, second

    def relay_x(first, second, half, relay, landing):
        arrive(first)

        def step(i, carry):
            half[to_right, i] = half[to_right, i] + relay[0, i]
            half[to_left, HALF + i] = half[to_left, HALF + i] + relay[1, i]
            return carry

        lax.fori_loop(0, HALF, step, 0)
        return second + [
            push(half.at[to_right, near], landing.at[0, near], right_x),
            push(half.at[to_left, far], landing.at[1, far], left_x),
        ]

    def send_x_direct(half, relay, landing):
        return [
            push(half.at[to_right], landing.at[0], right_x),
            push(half.at[to_left], landing.at[1], left_x),
            push(half.at[across], relay, across_x),
        ]

    def add_x_direct(half, relay, landing, eighth):
        def step(zz, carry):
            total = half[x, zz].astype(F32) + landing[0, zz].astype(F32)
            total = total + landing[1, zz].astype(F32) + relay[zz].astype(F32)
            eighth[zz] = total.astype(BF16)
            return carry

        lax.fori_loop(0, NZ, step, 0)

    def add_x(half, landing, eighth):
        def step(zz, carry):
            total = half[x, zz].astype(F32) + landing[0, zz].astype(F32) + landing[1, zz].astype(F32)
            eighth[zz] = total.astype(BF16)
            return carry

        lax.fori_loop(0, NZ, step, 0)

    def send_z(eighth, landing):
        return [push(eighth.at[lax.rem(z + d, NZ)], landing.at[d - 1], z_peers[d - 1]) for d in range(1, NZ)]

    def total_z(eighth, landing):
        total = eighth[z].astype(F32)
        for d in range(NZ - 1):
            total = total + landing[d].astype(F32)
        return total

    l_mesh.wait()
    xh, rstd_x = normalise(mesh_v[...])
    xhat[...] = xh
    mn[1] = xh.astype(BF16)
    l_qkv.wait()
    kv[1, 0] = dot_nn(mn[1], wqkv[1]).astype(BF16)
    kv[1, 1] = dot_nn(mn[1], wqkv[2]).astype(BF16)
    outer = lax.div(y, NY - 1) + lax.div(NY - 1 - y, NY - 1)
    pl.semaphore_wait(barrier, len(peers) + NY * outer)
    kv_copies = [push(kv.at[1], kv.at[0], above), push(kv.at[1], kv.at[2], below)]
    qp[...] = dot_nn(mn[1], wqkv[0]).astype(BF16)

    l_grid.wait()

    def grid_rows(i, carry):
        rows = pl.ds(pl.multiple_of(i * 64, 64), 64)
        gh, rstd = normalise(grid_v[rows, :])
        gn[rows, :] = gh.astype(BF16)
        grstd[rows, :] = jnp.broadcast_to(rstd, (64, 128))
        return carry

    lax.fori_loop(0, POINTS // 64, grid_rows, 0)
    l_dq.wait()
    qd[...] = dot_nn(gn[...], wdq[...]).astype(BF16)
    gn_t[...] = gn[...].T

    arrive(kv_copies)
    mn_copies = [push(mn.at[1], mn.at[0], above), push(mn.at[1], mn.at[2], below)]

    def stack_heads(block, h):
        kbd[h, block * ROWS : (block + 1) * ROWS, :] = kv[block, 0] * masks[h]
        vbd[h, block * ROWS : (block + 1) * ROWS, :] = kv[block, 1] * masks[h]

    for h in range(HEADS):
        for block in range(3):
            stack_heads(block, h)
    span = 3 * ROWS
    pt[...] = dot_nt(kbd[...].reshape(HEADS * span, COLS), qp[...]).reshape(HEADS, span, ROWS)
    key_row = lax.broadcasted_iota(jnp.int32, (span, ROWS), 0)
    query_row = lax.broadcasted_iota(jnp.int32, (span, ROWS), 1)
    position = band * ROWS - ROWS + key_row
    valid = (
        (key_row >= query_row) & (key_row <= query_row + 2 * WINDOW)
        & (position >= 0) & (position < BANDS * ROWS)
    )

    def window_softmax(h, carry):
        score = jnp.where(valid, pt[h] * FACTOR, NEG)
        weight = jnp.exp(score - jnp.max(score, axis=0, keepdims=True))
        pt[h] = weight / jnp.sum(weight, axis=0, keepdims=True)
        return carry

    lax.fori_loop(0, HEADS, window_softmax, 0)
    probs_b = pt[...].astype(BF16).reshape(HEADS * span, ROWS)
    attended[...] = dot_tn(probs_b, vbd[...].reshape(HEADS * span, COLS)).astype(BF16)
    l_po.wait()
    part1[...] = dot_nn(attended[...], wpo[...]).astype(BF16).reshape(NY, SHARE, D)
    copies = scatter_share(part1, part1_in)

    l_dout.wait()
    l_do.wait()
    ud[...] = dot_nt(dout_v[...], wdo[...]).astype(BF16)
    dout_t[...] = dout_v[...].T
    l_near.wait()
    l_count.wait()
    local = near_v[...] - band * ROWS
    count = count_v[...]

    def multiplicity(first, rows):
        mesh_row = lax.broadcasted_iota(jnp.int32, (rows, POINTS), 0) + first
        total = jnp.zeros((rows, POINTS), F32)
        for e in range(EDGES):
            hit = (local[e : e + 1] == mesh_row) & (count > e)
            total = total + jnp.where(hit, 1.0, 0.0)
        return total

    cc[...] = multiplicity(0, ROWS)
    cr[:RIM] = multiplicity(-RIM, RIM)
    cr[RIM:] = multiplicity(ROWS, RIM)

    arrive(copies)
    own_rows = pl.ds(pl.multiple_of(y * SHARE, SHARE), SHARE)
    state = (mesh_v[own_rows, :].astype(F32) + share_sum(part1, part1_in)).astype(BF16)
    yhat, rstd_y = normalise(state)
    sn[y] = yhat.astype(BF16)
    copies = gather_share(sn)

    def rim_copy(c, side):
        row, dst = ((0, RIM), (SHARE - RIM, 0))[side]
        return pltpu.make_async_remote_copy(
            src_ref=sn.at[y, pl.ds(row, RIM), :], dst_ref=sn.at[NY, pl.ds(dst, RIM), :],
            send_sem=rim_send.at[c], recv_sem=rim_recv.at[side],
            device_id=(lower, upper)[side][c], device_id_type=MESH,
        )

    @pl.when(y == 0)
    def _():
        for c in range(NY):
            rim_copy(c, 0).start()

    @pl.when(y == NY - 1)
    def _():
        for c in range(NY):
            rim_copy(c, 1).start()

    arrive(mn_copies)
    mn_t[...] = mn[...].reshape(3 * ROWS, D).T
    l_dkv.wait()
    arrive(copies)
    rim_copy(0, 0).wait_recv()
    rim_copy(0, 1).wait_recv()

    state_normed = sn[...].reshape(ROWS + 2 * RIM, D)
    sn_t[...] = state_normed.T
    own_kv[0] = dot_nn(state_normed, wdkv[0]).astype(BF16)
    own_kv[1] = dot_nn(state_normed, wdkv[1]).astype(BF16)
    for h in range(HEADS):
        kbd_c[h] = own_kv[0, :ROWS, :] * masks[h]
        vbd_c[h] = own_kv[1, :ROWS, :] * masks[h]
        kbd_r[h] = own_kv[0, ROWS:, :] * masks[h]
        vbd_r[h] = own_kv[1, ROWS:, :] * masks[h]
    s_c[...] = dot_nt(kbd_c[...].reshape(HEADS * ROWS, COLS), qd[...]).reshape(HEADS, ROWS, POINTS)
    dw_c[...] = dot_nt(vbd_c[...].reshape(HEADS * ROWS, COLS), ud[...]).reshape(HEADS, ROWS, POINTS)
    s_r[...] = dot_nt(kbd_r[...].reshape(HEADS * 2 * RIM, COLS), qd[...]).reshape(HEADS, 2 * RIM, POINTS)
    dw_r[...] = dot_nt(vbd_r[...].reshape(HEADS * 2 * RIM, COLS), ud[...]).reshape(HEADS, 2 * RIM, POINTS)

    def edge_softmax(h, carry):
        for lo in range(0, POINTS, 128):
            at_c, at_r = cc[:, lo : lo + 128], cr[:, lo : lo + 128]
            score_c = jnp.where(at_c > 0, s_c[h, :, lo : lo + 128] * FACTOR, NEG)
            score_r = jnp.where(at_r > 0, s_r[h, :, lo : lo + 128] * FACTOR, NEG)
            top = jnp.maximum(jnp.max(score_c, axis=0, keepdims=True), jnp.max(score_r, axis=0, keepdims=True))
            e_c = at_c * jnp.exp(score_c - top)
            e_r = at_r * jnp.exp(score_r - top)
            scale = 1.0 / (jnp.sum(e_c, axis=0, keepdims=True) + jnp.sum(e_r, axis=0, keepdims=True))
            e_c = e_c * scale
            e_r = e_r * scale
            d_c = dw_c[h, :, lo : lo + 128]
            d_r = dw_r[h, :, lo : lo + 128]
            centre = jnp.sum(e_c * d_c, axis=0, keepdims=True) + jnp.sum(e_r * d_r, axis=0, keepdims=True)
            w_c[h, :, lo : lo + 128] = e_c.astype(BF16)
            w_r[h, :, lo : lo + 128] = e_r.astype(BF16)
            ds_c[h, :, lo : lo + 128] = (e_c * (d_c - centre) * FACTOR).astype(BF16)
            ds_r[h, :, lo : lo + 128] = (e_r * (d_r - centre) * FACTOR).astype(BF16)
        return carry

    lax.fori_loop(0, HEADS, edge_softmax, 0)

    def own_head(product, rows):
        blocks = product.reshape(HEADS, rows, COLS)
        total = lax.index_in_dim(blocks, 0, 0, keepdims=False) * masks_f[0]
        for h in range(1, HEADS):
            total = total + lax.index_in_dim(blocks, h, 0, keepdims=False) * masks_f[h]
        return total

    def flat(ref):
        return ref[...].reshape(ref.shape[0] * ref.shape[1], ref.shape[2])

    for which, (upstream_c, upstream_r, right) in enumerate(((ds_c, ds_r, qd), (w_c, w_r, ud))):
        cols = slice(which * COLS, (which + 1) * COLS)
        dkv_ext[:ROWS, cols] = own_head(dot_nn(flat(upstream_c), right[...]), ROWS).astype(BF16)
        dkv_ext[ROWS:, cols] = own_head(dot_nn(flat(upstream_r), right[...]), 2 * RIM).astype(BF16)
    part2[...] = (
        (dot_nt(dkv_ext[:, :COLS], wdkv[0]) + dot_nt(dkv_ext[:, COLS:], wdkv[1]))
        .astype(BF16).reshape(NY + 1, SHARE, D)
    )
    copies = scatter_share(part2, part2_in)

    def rim2_copy(side, slot):
        return pltpu.make_async_remote_copy(
            src_ref=part2.at[NY, pl.ds(side * RIM, RIM), :], dst_ref=rim2_in.at[slot],
            send_sem=rim2_send.at[side], recv_sem=rim2_recv.at[slot],
            device_id=(lower[NY - 1], upper[0])[side], device_id_type=MESH,
        )

    rim2_copy(0, y).start()
    rim2_copy(1, y).start()

    dec[...] = (dot_tn(flat(w_c), flat(vbd_c)) + dot_tn(flat(w_r), flat(vbd_r))).astype(BF16)
    dq[...] = (dot_tn(flat(ds_c), flat(kbd_c)) + dot_tn(flat(ds_r), flat(kbd_r))).astype(BF16)

    store_grad(ga, 0, gn_t, dq[...])
    paira = send_pair(ga, raa)
    store_grad(g0, 0, dout_t, dec[...])
    pair0 = send_pair(g0, ra0)
    store_grad(g1, 0, sn_t, dkv_ext[...])
    pair1 = send_pair(g1, ra1)

    arrive(copies)
    share[...] = share_sum(part2, part2_in)

    def rim_sum():
        for c in range(NY):
            rim2_copy(0, c).wait_recv()
        total = rim2_in[0].astype(F32)
        for c in range(1, NY):
            total = total + rim2_in[c].astype(F32)
        return total

    @pl.when(y == 0)
    def _():
        share[:RIM, :] = share[:RIM, :] + rim_sum()

    @pl.when(y == NY - 1)
    def _():
        share[SHARE - RIM :, :] = share[SHARE - RIM :, :] + rim_sum()

    sgrad[...] = normalise_back(yhat, rstd_y, share[...])
    sg[y] = sgrad[...].astype(BF16)
    copies = gather_share(sg)
    arrive(paira)
    add_pair_z(ga, raa, hba)
    za = send_z(hba, rza)
    arrive(pair0)
    add_pair(g0, ra0, hb0)
    x0 = send_x(hb0, ry0, rb0)

    def grid_part(i, carry):
        rows = pl.ds(pl.multiple_of(i * 128, 128), 128)
        half_rows = pl.ds(pl.multiple_of(lax.rem(i, 2) * 128, 128), 128)
        half = lax.div(i, 2)
        value = dot_nt(dq[rows, :], wdq[...])
        first = jnp.mean(value, axis=-1, keepdims=True)
        second = jnp.mean(value * gn[rows, :].astype(F32), axis=-1, keepdims=True)
        lane = lax.broadcasted_iota(jnp.int32, (128, 128), 1)
        both = jnp.where(lane == 0, first, jnp.where(lane == 1, second, 0.0)).T
        gstat[i] = both[:8]
        for q in range(NY):
            gb[half, q, half_rows, :] = value[:, q * COLS : (q + 1) * COLS].astype(BF16)
        return carry

    lax.fori_loop(0, POINTS // 128, grid_part, 0)

    def send_grid(half):
        return [
            push(gb.at[half, lax.rem(y + d, NY)], gb_in.at[half, d - 1], y_peers[d - 1]) for d in range(1, NY)
        ]

    arrive(pair1)
    add_pair(g1, ra1, hb1)
    x1 = send_x(hb1, ry1, rb1)
    x0 = relay_x(*x0, hb0, ry0, rb0)

    arrive(copies)
    grid_copies = send_grid(0)
    x1 = relay_x(*x1, hb1, ry1, rb1)
    state_grad_b = sg[...].reshape(ROWS, D)
    da = dot_nt(state_grad_b, wpo[...]).astype(BF16)
    dpt[...] = dot_nt(vbd[...].reshape(HEADS * span, COLS), da).reshape(HEADS, span, ROWS)

    def window_back(h, carry):
        prob = pt[h]
        dprob = dpt[h]
        centre = jnp.sum(prob * dprob, axis=0, keepdims=True)
        dpt[h] = prob * (dprob - centre)
        return carry

    lax.fori_loop(0, HEADS, window_back, 0)
    dscore = dpt[...].astype(BF16).reshape(HEADS * span, ROWS)
    dk_ext = own_head(dot_nn(dscore, qp[...]), span) * FACTOR
    dv_ext = own_head(dot_nn(pt[...].astype(BF16).reshape(HEADS * span, ROWS), da), span)
    for which, ext in ((0, dk_ext), (1, dv_ext)):
        rounded = ext.astype(BF16)
        dkv3[:, which * COLS : (which + 1) * COLS] = rounded
        ring_out[0, which] = rounded[:ROWS]
        ring_out[1, which] = rounded[2 * ROWS :]
    ring_copies = [push(ring_out.at[0], ring_in.at[0], below), push(ring_out.at[1], ring_in.at[1], above)]
    settled = len(used)
    store_grad(g2, 0, mn_t, dkv3[...])
    pair2 = send_pair(g2, ra2)
    dqkv[:, :COLS] = (
        dot_tn(dscore, kbd[...].reshape(HEADS * span, COLS)) * FACTOR
    ).astype(BF16)
    mn_own_t[...] = mn_t[:, ROWS : 2 * ROWS]
    store_grad(gq, 0, mn_own_t, dqkv[:, :COLS])
    pairq = send_pair(gq, raq)
    sg_t[...] = state_grad_b.T
    store_grad(g3, 0, sg_t, attended[...])
    pair3 = send_pair(g3, ra3)

    arrive(ring_copies)
    for which, ext in ((0, dk_ext), (1, dv_ext)):
        total = ext[ROWS : 2 * ROWS] + ring_in[0, which].astype(F32) + ring_in[1, which].astype(F32)
        dqkv[:, (which + 1) * COLS : (which + 2) * COLS] = total.astype(BF16)
    part3[...] = (
        (
            dot_nt(dqkv[:, :COLS], wqkv[0])
            + dot_nt(dqkv[:, COLS : 2 * COLS], wqkv[1])
            + dot_nt(dqkv[:, 2 * COLS :], wqkv[2])
        ).astype(BF16).reshape(NY, SHARE, D)
    )
    copies = scatter_share(part3, part3_in)

    arrive(pair2)
    add_pair(g2, ra2, hb2)
    x2 = send_x_direct(hb2, ry2, rb2)
    arrive(pairq)
    add_pair_z(gq, raq, hbq)
    zq = send_z(hbq, rzq)
    arrive(pair3)
    add_pair(g3, ra3, hb3)
    x3 = send_x_direct(hb3, ry3, rb3)

    arrive(copies)
    own_x = xhat[own_rows, :]
    centred, rstd_own = normalise(mesh_v[own_rows, :])
    result = sgrad[...] + normalise_back(own_x, rstd_own, share_sum(part3, part3_in))
    back[y] = result.astype(BF16)
    back_copies = gather_share(back)
    grid_copies += send_grid(1)
    for d in range(1, NY):
        grid_copies.append(push(gstat, gstat_in.at[d - 1], y_peers[d - 1]))

    arrive(za)
    add_z(hba, rza, hca)
    xa = send_x_last(hca, rxa)
    arrive(x0)
    add_x(hb0, rb0, hc0)
    z0 = send_z(hc0, rc0)
    arrive(x1)
    add_x(hb1, rb1, hc1)
    z1 = send_z(hc1, rc1)

    for copy in used[:settled]:
        copy.wait_send()
    arrive(x2)
    add_x_direct(hb2, ry2, rb2, hc2)
    z2 = send_z(hc2, rc2)
    arrive(zq)
    add_z(hbq, rzq, hcq)
    xq = send_x_last(hcq, rxq)
    arrive(x3)
    add_x_direct(hb3, ry3, rb3, hc3)
    z3 = send_z(hc3, rc3)

    arrive(grid_copies)
    columns = pl.ds(pl.multiple_of(y * COLS, COLS), COLS)

    def grid_final(i, carry):
        rows = pl.ds(pl.multiple_of(i * 128, 128), 128)
        stat = gstat[i]
        half_rows = pl.ds(pl.multiple_of(lax.rem(i, 2) * 128, 128), 128)
        half = lax.div(i, 2)
        value = gb[half, y, half_rows, :].astype(F32)
        for d in range(NY - 1):
            stat = stat + gstat_in[d, i]
            value = value + gb_in[half, d, half_rows, :].astype(F32)
        stat = jnp.concatenate([stat, jnp.zeros((120, 128), F32)], axis=0).T
        change = value - stat[:, 0:1] - gn[rows, columns].astype(F32) * stat[:, 1:2]
        out_grid[rows, :] = (dout_v[rows, columns].astype(F32) + grstd[rows, 0:1] * change).astype(BF16)
        return carry

    lax.fori_loop(0, POINTS // 128, grid_final, 0)
    arrive(back_copies)
    out_mesh[...] = back[...].reshape(ROWS, D)

    arrive(z0)
    out_do[...] = total_z(hc0, rc0)
    arrive(xa)
    out_dq[...] = total_x(hca, rxa)
    arrive(z1)
    total = total_z(hc1, rc1)
    out_dkv[0] = total[:PART]
    out_dkv[1] = total[PART:]
    arrive(z2)
    total = total_z(hc2, rc2)
    out_qkv[1] = total[:PART]
    out_qkv[2] = total[PART:]
    arrive(xq)
    out_qkv[0] = total_x(hcq, rxq)
    arrive(z3)
    out_po[...] = total_z(hc3, rc3)
    rim2_copy(0, 0).wait_send()
    rim2_copy(1, 0).wait_send()

    @pl.when((y == 0) | (y == NY - 1))
    def _():
        for c in range(NY):
            rim_copy(c, 0).wait_send()

    for copy in used[settled:]:
        copy.wait_send()


def copy_out(*refs):
    count = len(refs) // 2
    for source, target in zip(refs[:count], refs[count:]):
        target[...] = source[...]


def body(
    mesh_node_state, grid_state, d_out, neighbours, edge_count, w_proc_qkv, w_proc_out, w_dec_q, w_dec_kv, w_dec_out
):
    span = 3 * ROWS
    v = pltpu.VMEM

    def reduce_scratch(make):
        return [make(n * PART) for n in GROUPS]

    scratch = [
        v((ROWS, D), BF16), v((POINTS, D), BF16), v((POINTS, D), BF16), v((EDGES, POINTS), jnp.int32),
        v((1, POINTS), jnp.int32), v((3, D, COLS), BF16), v((COLS, D), BF16), v((D, COLS), BF16),
        v((2, D, COLS), BF16), v((COLS, D), BF16),
        v((ROWS, D), F32), v((3, ROWS, D), BF16), v((D, span), BF16), v((D, ROWS), BF16), v((D, ROWS + 2 * RIM), BF16), v((D, ROWS), BF16), v((3, 2, ROWS, COLS), BF16), v((ROWS, COLS), BF16),
        v((HEADS, span, COLS), BF16), v((HEADS, span, COLS), BF16), v((HEADS, span, ROWS), F32),
        v((HEADS, span, ROWS), F32), v((ROWS, COLS), BF16),
        v((NY, SHARE, D), BF16), v((NY - 1, SHARE, D), BF16), v((NY + 1, SHARE, D), BF16), v((POINTS, D), BF16),
        v((D, POINTS), BF16), v((D, POINTS), BF16), v((POINTS, 128), F32), v((POINTS, COLS), BF16),
        v((POINTS, COLS), BF16),
        v((2, ROWS + 2 * RIM, COLS), BF16),
        v((HEADS, ROWS, COLS), BF16), v((HEADS, ROWS, COLS), BF16),
        v((HEADS, 2 * RIM, COLS), BF16), v((HEADS, 2 * RIM, COLS), BF16),
        v((ROWS, POINTS), F32), v((2 * RIM, POINTS), F32),
        v((HEADS, ROWS, POINTS), F32), v((HEADS, 2 * RIM, POINTS), F32),
        v((HEADS, ROWS, POINTS), F32), v((HEADS, 2 * RIM, POINTS), F32),
        v((HEADS, ROWS, POINTS), BF16), v((HEADS, 2 * RIM, POINTS), BF16),
        v((HEADS, ROWS, POINTS), BF16), v((HEADS, 2 * RIM, POINTS), BF16),
        v((ROWS + 2 * RIM, 2 * COLS), BF16),
        v((POINTS, COLS), BF16), v((POINTS, COLS), BF16), v((2, NY, POINTS // 2, COLS), BF16),
        v((2, NY - 1, POINTS // 2, COLS), BF16), v((POINTS // 128, 8, 128), F32), v((NY - 1, POINTS // 128, 8, 128), F32),
        v((NY + 1, SHARE, D), BF16), v((NY - 1, SHARE, D), BF16), v((NY, RIM, D), BF16), v((SHARE, D), F32),
        v((SHARE, D), F32), v((NY, SHARE, D), BF16),
        v((2, 2, ROWS, COLS), BF16), v((2, 2, ROWS, COLS), BF16),
        v((span, 2 * COLS), BF16), v((ROWS, 3 * COLS), BF16),
        v((NY, SHARE, D), BF16), v((NY - 1, SHARE, D), BF16), v((NY, SHARE, D), BF16),
    ]
    scratch += reduce_scratch(lambda r: v((NC, NX, NZ, r, COLS), BF16))
    scratch += reduce_scratch(lambda r: v((NX, NZ, r, COLS), BF16))
    scratch += reduce_scratch(lambda r: v((NX, NZ, r, COLS), BF16))
    scratch += reduce_scratch(lambda r: v((2, HALF, r, COLS), BF16))[:2]
    scratch += reduce_scratch(lambda r: v((NZ, r, COLS), BF16))[2:]
    scratch += reduce_scratch(lambda r: v((2, NZ, r, COLS), BF16))
    scratch += reduce_scratch(lambda r: v((NZ, r, COLS), BF16))
    scratch += reduce_scratch(lambda r: v((NZ - 1, r, COLS), BF16))
    chunk = (PART, COLS)
    for lead in ((NC, NX, NZ), (NX, NZ), (NZ, NX), (NZ - 1, NX), (NX,), (NX - 1,)):
        scratch += [v(lead + chunk, BF16), v(lead + chunk, BF16)]
    scratch += [
        pltpu.SemaphoreType.DMA((10,)), pltpu.SemaphoreType.DMA((REMOTE,)), pltpu.SemaphoreType.DMA((REMOTE,)),
        pltpu.SemaphoreType.DMA((NY,)), pltpu.SemaphoreType.DMA((2,)), pltpu.SemaphoreType.DMA((2,)),
        pltpu.SemaphoreType.DMA((NY,)),
    ]
    shapes = (
        ((ROWS, D), BF16), ((POINTS, COLS), BF16), ((3, PART, COLS), F32), ((PART, COLS), F32),
        ((PART, COLS), F32), ((2, PART, COLS), F32), ((PART, COLS), F32),
    )
    results = pl.pallas_call(
        kernel,
        out_shape=[jax.ShapeDtypeStruct(shape, kind) for shape, kind in shapes],
        in_specs=[pl.BlockSpec(memory_space=pl.ANY)] * 10,
        out_specs=[pl.BlockSpec(memory_space=pltpu.VMEM)] * 7,
        scratch_shapes=scratch,
        compiler_params=pltpu.CompilerParams(
            collective_id=0, has_side_effects=True, vmem_limit_bytes=56 * 2**20
        ),
    )(
        mesh_node_state, grid_state, d_out, neighbours.T, edge_count.reshape(1, POINTS),
        w_proc_qkv, w_proc_out, w_dec_q, w_dec_kv, w_dec_out,
    )
    mesh_grad, grid_grad, g_qkv, g_po, g_dq, g_dkv, g_do = pl.pallas_call(
        copy_out,
        out_shape=[jax.ShapeDtypeStruct(shape, kind) for shape, kind in shapes],
        in_specs=[pl.BlockSpec(memory_space=pltpu.VMEM)] * 7,
        out_specs=[pl.BlockSpec(memory_space=pltpu.VMEM)] * 7,
    )(*results)
    return mesh_grad, grid_grad, g_qkv, g_po.T, g_dq, g_dkv, g_do.T


def solution(mesh):
    placed = (
        P("band", None), P("band", None), P("band", None), P("band", None), P("band"),
        P(None, None, "chan"), P("chan", None), P(None, "chan"), P(None, None, "chan"), P("chan", None),
    )
    return jax.shard_map(
        body,
        mesh=mesh,
        in_specs=placed,
        out_specs=(
            P("band", None), P("band", "chan"), P(None, "band", "chan"), P("chan", "band"),
            P("band", "chan"), P(None, "band", "chan"), P("chan", "band"),
        ),
        check_vma=False,
    )
```

```python
import jax
import jax.numpy as jnp
from jax import lax
from jax.experimental import pallas as pl
from jax.experimental.pallas import tpu as pltpu
from jax.sharding import PartitionSpec as P

NZ, NX, NC, NY = 8, 4, 2, 4
BANDS = NZ * NX * NC
D = 1024
ROWS = 128
POINTS = 512
COLS = 256
HEADS = 4
HEAD_DIM = 64
EDGES = 4
RIM = 16
WINDOW = 128
SHARE = ROWS // NY
PART = D // BANDS
EPS = 1e-05
NEG = -1e30
FACTOR = HEAD_DIM**-0.5
F32 = jnp.float32
BF16 = jnp.bfloat16
MESH = pl.DeviceIdType.MESH
GROUPS = (1, 2, 2, 1)
HALF = NZ // 2
REMOTE = 128


def dot_nn(a, b):
    return lax.dot_general(a, b, (((1,), (0,)), ((), ())), preferred_element_type=F32)


def dot_nt(a, b):
    return lax.dot_general(a, b, (((1,), (1,)), ((), ())), preferred_element_type=F32)


def dot_tn(a, b):
    return lax.dot_general(a, b, (((0,), (0,)), ((), ())), preferred_element_type=F32)


def normalise(values):
    values = values.astype(F32)
    centre = jnp.mean(values, axis=-1, keepdims=True)
    shifted = values - centre
    rstd = lax.rsqrt(jnp.mean(shifted * shifted, axis=-1, keepdims=True) + EPS)
    return shifted * rstd, rstd


def normalise_back(normed, rstd, upstream):
    first = jnp.mean(upstream, axis=-1, keepdims=True)
    second = jnp.mean(upstream * normed, axis=-1, keepdims=True)
    return rstd * (upstream - first - normed * second)


def head_masks(dtype):
    lane = lax.broadcasted_iota(jnp.int32, (1, COLS), 1)
    return [((lane >= h * HEAD_DIM) & (lane < (h + 1) * HEAD_DIM)).astype(F32).astype(dtype) for h in range(HEADS)]


def kernel(
    mesh_hbm, grid_hbm, dout_hbm, near_hbm, count_hbm, wqkv_hbm, wpo_hbm, wdq_hbm, wdkv_hbm, wdo_hbm,
    out_mesh, out_grid, out_qkv, out_po, out_dq, out_dkv, out_do,
    mesh_v, grid_v, dout_v, near_v, count_v, wqkv, wpo, wdq, wdkv, wdo,
    xhat, mn, mn_t, mn_own_t, sn_t, sg_t, kv, qp, kbd, vbd, pt, dpt, attended,
    part1, part1_in, sn, gn, gn_t, dout_t, grstd, qd, ud,
    own_kv, kbd_c, vbd_c, kbd_r, vbd_r, cc, cr, s_c, s_r, dw_c, dw_r, w_c, w_r, ds_c, ds_r,
    dkv_ext, dec, dq, gb, gb_in, gstat, gstat_in,
    part2, part2_in, rim2_in, share, sgrad, sg, ring_out, ring_in, dkv3, dqkv, part3, part3_in, back,
    g0, g1, g2, g3, ra0, ra1, ra2, ra3, hb0, hb1, hb2, hb3, ry0, ry1, ry2, ry3,
    rb0, rb1, rb2, rb3, hc0, hc1, hc2, hc3, rc0, rc1, rc2, rc3,
    ga, gq, raa, raq, hba, hbq, rza, rzq, hca, hcq, rxa, rxq,
    load_sem, send_sem, recv_sem, rim_send, rim_recv, rim2_send, rim2_recv,
):
    band = lax.axis_index("band")
    y = lax.axis_index("chan")
    core = lax.rem(band, NC)
    x = lax.rem(lax.div(band, NC), NX)
    z = lax.div(band, NC * NX)

    def at(zz, xx, c):
        return {"band": (zz * NX + xx) * NC + c}

    pair = at(z, x, 1 - core)
    x_peers = [at(z, lax.rem(x + d, NX), core) for d in range(1, NX)]
    across_x = x_peers[1]
    z_peers = [at(lax.rem(z + d, NZ), x, core) for d in range(1, NZ)]
    y_peers = [{"chan": lax.rem(y + d, NY)} for d in range(1, NY)]
    above = {"band": lax.rem(band + 1, BANDS)}
    below = {"band": lax.rem(band + BANDS - 1, BANDS)}

    lower = [{"band": (band + BANDS - 1) % BANDS, "chan": c} for c in range(NY)]
    upper = [{"band": (band + 1) % BANDS, "chan": c} for c in range(NY)]

    barrier = pltpu.get_barrier_semaphore()

    def greet(peers):
        for peer in peers:
            pl.semaphore_signal(barrier, inc=1, device_id=peer, device_id_type=MESH)

    peers = [pair, above, below, lower[NY - 1], upper[0]] + x_peers + y_peers + z_peers
    greet(peers)

    @pl.when(y == 0)
    def _():
        greet(lower)

    @pl.when(y == NY - 1)
    def _():
        greet(upper)

    loads = []
    for i, (src, dst) in enumerate((
        (mesh_hbm, mesh_v), (wqkv_hbm, wqkv), (grid_hbm, grid_v), (wdq_hbm, wdq), (dout_hbm, dout_v), (wdo_hbm, wdo),
        (near_hbm, near_v), (count_hbm, count_v), (wpo_hbm, wpo), (wdkv_hbm, wdkv),
    )):
        load = pltpu.make_async_copy(src, dst, load_sem.at[i])
        load.start()
        loads.append(load)
    l_mesh, l_qkv, l_grid, l_dq, l_dout, l_do, l_near, l_count, l_po, l_dkv = loads

    used = []

    def push(src, dst, peer):
        slot = len(used)
        copy = pltpu.make_async_remote_copy(
            src_ref=src, dst_ref=dst, send_sem=send_sem.at[slot], recv_sem=recv_sem.at[slot],
            device_id=peer, device_id_type=MESH,
        )
        copy.start()
        used.append(copy)
        return copy

    def arrive(copies):
        for copy in copies:
            copy.wait_recv()

    masks = head_masks(BF16)
    masks_f = head_masks(F32)

    def scatter_share(partial, landing):
        return [push(partial.at[lax.rem(y + d, NY)], landing.at[d - 1], y_peers[d - 1]) for d in range(1, NY)]

    def gather_share(blocks):
        return [push(blocks.at[y], blocks.at[y], y_peers[d - 1]) for d in range(1, NY)]

    def share_sum(partial, landing):
        total = partial[y].astype(F32)
        for d in range(NY - 1):
            total = total + landing[d].astype(F32)
        return total

    def store_grad(group, first, left_t, right):
        width = right.shape[1] // COLS

        def rows(zz, carry):
            lhs = left_t[pl.ds(pl.multiple_of(zz * ROWS, ROWS), ROWS), :]
            value = dot_nn(lhs, right).astype(BF16)
            for xx in range(NX):
                for c in range(NC):
                    lo = (xx * NC + c) * PART
                    for m in range(width):
                        group[c, xx, zz, (first + m) * PART : (first + m + 1) * PART, :] = value[
                            lo : lo + PART, m * COLS : (m + 1) * COLS
                        ]
            return carry

        lax.fori_loop(0, NZ, rows, 0)

    def send_pair(group, landing):
        return [push(group.at[1 - core], landing, pair)]

    def add_pair(group, landing, half):
        def step(xx, carry):
            for zz in range(NZ):
                half[xx, zz] = group[core, xx, zz] + landing[xx, zz]
            return carry

        lax.fori_loop(0, NX, step, 0)

    def add_pair_z(group, landing, half):
        def step(xx, carry):
            for zz in range(NZ):
                half[zz, xx] = group[core, xx, zz] + landing[xx, zz]
            return carry

        lax.fori_loop(0, NX, step, 0)

    def add_z(half, landing, eighth):
        for xx in range(NX):
            total = half[z, xx].astype(F32)
            for d in range(NZ - 1):
                total = total + landing[d, xx].astype(F32)
            eighth[xx] = total.astype(BF16)

    def send_x_last(eighth, landing):
        return [push(eighth.at[lax.rem(x + d, NX)], landing.at[d - 1], x_peers[d - 1]) for d in range(1, NX)]

    def total_x(eighth, landing):
        total = eighth[x].astype(F32)
        for d in range(NX - 1):
            total = total + landing[d].astype(F32)
        return total

    right_x, left_x = at(z, lax.rem(x + 1, NX), core), at(z, lax.rem(x + NX - 1, NX), core)
    to_right, to_left, across = lax.rem(x + 1, NX), lax.rem(x + NX - 1, NX), lax.rem(x + 2, NX)
    near, far = pl.ds(0, HALF), pl.ds(HALF, HALF)

    def send_x(half, relay, landing):
        first = [
            push(half.at[across, near], relay.at[0], right_x),
            push(half.at[across, far], relay.at[1], left_x),
        ]
        second = [
            push(half.at[to_right, far], landing.at[0, far], right_x),
            push(half.at[to_left, near], landing.at[1, near], left_x),
        ]
        return first, second

    def relay_x(first, second, half, relay, landing):
        arrive(first)

        def step(i, carry):
            half[to_right, i] = half[to_right, i] + relay[0, i]
            half[to_left, HALF + i] = half[to_left, HALF + i] + relay[1, i]
            return carry

        lax.fori_loop(0, HALF, step, 0)
        return second + [
            push(half.at[to_right, near], landing.at[0, near], right_x),
            push(half.at[to_left, far], landing.at[1, far], left_x),
        ]

    def send_x_direct(half, relay, landing):
        return [
            push(half.at[to_right], landing.at[0], right_x),
            push(half.at[to_left], landing.at[1], left_x),
            push(half.at[across], relay, across_x),
        ]

    def add_x_direct(half, relay, landing, eighth):
        def step(zz, carry):
            total = half[x, zz].astype(F32) + landing[0, zz].astype(F32)
            total = total + landing[1, zz].astype(F32) + relay[zz].astype(F32)
            eighth[zz] = total.astype(BF16)
            return carry

        lax.fori_loop(0, NZ, step, 0)

    def add_x(half, landing, eighth):
        def step(zz, carry):
            total = half[x, zz].astype(F32) + landing[0, zz].astype(F32) + landing[1, zz].astype(F32)
            eighth[zz] = total.astype(BF16)
            return carry

        lax.fori_loop(0, NZ, step, 0)

    def send_z(eighth, landing):
        return [push(eighth.at[lax.rem(z + d, NZ)], landing.at[d - 1], z_peers[d - 1]) for d in range(1, NZ)]

    def total_z(eighth, landing):
        total = eighth[z].astype(F32)
        for d in range(NZ - 1):
            total = total + landing[d].astype(F32)
        return total

    l_mesh.wait()
    xh, rstd_x = normalise(mesh_v[...])
    xhat[...] = xh
    mn[1] = xh.astype(BF16)
    l_qkv.wait()
    kv[1, 0] = dot_nn(mn[1], wqkv[1]).astype(BF16)
    kv[1, 1] = dot_nn(mn[1], wqkv[2]).astype(BF16)
    outer = lax.div(y, NY - 1) + lax.div(NY - 1 - y, NY - 1)
    pl.semaphore_wait(barrier, len(peers) + NY * outer)
    kv_copies = [push(kv.at[1], kv.at[0], above), push(kv.at[1], kv.at[2], below)]
    qp[...] = dot_nn(mn[1], wqkv[0]).astype(BF16)

    l_grid.wait()

    def grid_rows(i, carry):
        rows = pl.ds(pl.multiple_of(i * 64, 64), 64)
        gh, rstd = normalise(grid_v[rows, :])
        gn[rows, :] = gh.astype(BF16)
        grstd[rows, :] = jnp.broadcast_to(rstd, (64, 128))
        return carry

    lax.fori_loop(0, POINTS // 64, grid_rows, 0)
    l_dq.wait()
    qd[...] = dot_nn(gn[...], wdq[...]).astype(BF16)
    gn_t[...] = gn[...].T

    arrive(kv_copies)
    mn_copies = [push(mn.at[1], mn.at[0], above), push(mn.at[1], mn.at[2], below)]

    def stack_heads(block, h):
        kbd[h, block * ROWS : (block + 1) * ROWS, :] = kv[block, 0] * masks[h]
        vbd[h, block * ROWS : (block + 1) * ROWS, :] = kv[block, 1] * masks[h]

    for h in range(HEADS):
        for block in range(3):
            stack_heads(block, h)
    span = 3 * ROWS
    pt[...] = dot_nt(kbd[...].reshape(HEADS * span, COLS), qp[...]).reshape(HEADS, span, ROWS)
    key_row = lax.broadcasted_iota(jnp.int32, (span, ROWS), 0)
    query_row = lax.broadcasted_iota(jnp.int32, (span, ROWS), 1)
    position = band * ROWS - ROWS + key_row
    valid = (
        (key_row >= query_row) & (key_row <= query_row + 2 * WINDOW)
        & (position >= 0) & (position < BANDS * ROWS)
    )

    def window_softmax(h, carry):
        score = jnp.where(valid, pt[h] * FACTOR, NEG)
        weight = jnp.exp(score - jnp.max(score, axis=0, keepdims=True))
        pt[h] = weight / jnp.sum(weight, axis=0, keepdims=True)
        return carry

    lax.fori_loop(0, HEADS, window_softmax, 0)
    probs_b = pt[...].astype(BF16).reshape(HEADS * span, ROWS)
    attended[...] = dot_tn(probs_b, vbd[...].reshape(HEADS * span, COLS)).astype(BF16)
    l_po.wait()
    part1[...] = dot_nn(attended[...], wpo[...]).astype(BF16).reshape(NY, SHARE, D)
    copies = scatter_share(part1, part1_in)

    l_dout.wait()
    l_do.wait()
    ud[...] = dot_nt(dout_v[...], wdo[...]).astype(BF16)
    dout_t[...] = dout_v[...].T
    l_near.wait()
    l_count.wait()
    local = near_v[...] - band * ROWS
    count = count_v[...]

    def multiplicity(first, rows):
        mesh_row = lax.broadcasted_iota(jnp.int32, (rows, POINTS), 0) + first
        total = jnp.zeros((rows, POINTS), F32)
        for e in range(EDGES):
            hit = (local[e : e + 1] == mesh_row) & (count > e)
            total = total + jnp.where(hit, 1.0, 0.0)
        return total

    cc[...] = multiplicity(0, ROWS)
    cr[:RIM] = multiplicity(-RIM, RIM)
    cr[RIM:] = multiplicity(ROWS, RIM)

    arrive(copies)
    own_rows = pl.ds(pl.multiple_of(y * SHARE, SHARE), SHARE)
    state = (mesh_v[own_rows, :].astype(F32) + share_sum(part1, part1_in)).astype(BF16)
    yhat, rstd_y = normalise(state)
    sn[y] = yhat.astype(BF16)
    copies = gather_share(sn)

    def rim_copy(c, side):
        row, dst = ((0, RIM), (SHARE - RIM, 0))[side]
        return pltpu.make_async_remote_copy(
            src_ref=sn.at[y, pl.ds(row, RIM), :], dst_ref=sn.at[NY, pl.ds(dst, RIM), :],
            send_sem=rim_send.at[c], recv_sem=rim_recv.at[side],
            device_id=(lower, upper)[side][c], device_id_type=MESH,
        )

    @pl.when(y == 0)
    def _():
        for c in range(NY):
            rim_copy(c, 0).start()

    @pl.when(y == NY - 1)
    def _():
        for c in range(NY):
            rim_copy(c, 1).start()

    arrive(mn_copies)
    mn_t[...] = mn[...].reshape(3 * ROWS, D).T
    l_dkv.wait()
    arrive(copies)
    rim_copy(0, 0).wait_recv()
    rim_copy(0, 1).wait_recv()

    state_normed = sn[...].reshape(ROWS + 2 * RIM, D)
    sn_t[...] = state_normed.T
    own_kv[0] = dot_nn(state_normed, wdkv[0]).astype(BF16)
    own_kv[1] = dot_nn(state_normed, wdkv[1]).astype(BF16)
    for h in range(HEADS):
        kbd_c[h] = own_kv[0, :ROWS, :] * masks[h]
        vbd_c[h] = own_kv[1, :ROWS, :] * masks[h]
        kbd_r[h] = own_kv[0, ROWS:, :] * masks[h]
        vbd_r[h] = own_kv[1, ROWS:, :] * masks[h]
    s_c[...] = dot_nt(kbd_c[...].reshape(HEADS * ROWS, COLS), qd[...]).reshape(HEADS, ROWS, POINTS)
    dw_c[...] = dot_nt(vbd_c[...].reshape(HEADS * ROWS, COLS), ud[...]).reshape(HEADS, ROWS, POINTS)
    s_r[...] = dot_nt(kbd_r[...].reshape(HEADS * 2 * RIM, COLS), qd[...]).reshape(HEADS, 2 * RIM, POINTS)
    dw_r[...] = dot_nt(vbd_r[...].reshape(HEADS * 2 * RIM, COLS), ud[...]).reshape(HEADS, 2 * RIM, POINTS)

    def edge_softmax(h, carry):
        for lo in range(0, POINTS, 128):
            at_c, at_r = cc[:, lo : lo + 128], cr[:, lo : lo + 128]
            score_c = jnp.where(at_c > 0, s_c[h, :, lo : lo + 128] * FACTOR, NEG)
            score_r = jnp.where(at_r > 0, s_r[h, :, lo : lo + 128] * FACTOR, NEG)
            top = jnp.maximum(jnp.max(score_c, axis=0, keepdims=True), jnp.max(score_r, axis=0, keepdims=True))
            e_c = at_c * jnp.exp(score_c - top)
            e_r = at_r * jnp.exp(score_r - top)
            scale = 1.0 / (jnp.sum(e_c, axis=0, keepdims=True) + jnp.sum(e_r, axis=0, keepdims=True))
            e_c = e_c * scale
            e_r = e_r * scale
            d_c = dw_c[h, :, lo : lo + 128]
            d_r = dw_r[h, :, lo : lo + 128]
            centre = jnp.sum(e_c * d_c, axis=0, keepdims=True) + jnp.sum(e_r * d_r, axis=0, keepdims=True)
            w_c[h, :, lo : lo + 128] = e_c.astype(BF16)
            w_r[h, :, lo : lo + 128] = e_r.astype(BF16)
            ds_c[h, :, lo : lo + 128] = (e_c * (d_c - centre) * FACTOR).astype(BF16)
            ds_r[h, :, lo : lo + 128] = (e_r * (d_r - centre) * FACTOR).astype(BF16)
        return carry

    lax.fori_loop(0, HEADS, edge_softmax, 0)

    def own_head(product, rows):
        blocks = product.reshape(HEADS, rows, COLS)
        total = lax.index_in_dim(blocks, 0, 0, keepdims=False) * masks_f[0]
        for h in range(1, HEADS):
            total = total + lax.index_in_dim(blocks, h, 0, keepdims=False) * masks_f[h]
        return total

    def flat(ref):
        return ref[...].reshape(ref.shape[0] * ref.shape[1], ref.shape[2])

    for which, (upstream_c, upstream_r, right) in enumerate(((ds_c, ds_r, qd), (w_c, w_r, ud))):
        cols = slice(which * COLS, (which + 1) * COLS)
        dkv_ext[:ROWS, cols] = own_head(dot_nn(flat(upstream_c), right[...]), ROWS).astype(BF16)
        dkv_ext[ROWS:, cols] = own_head(dot_nn(flat(upstream_r), right[...]), 2 * RIM).astype(BF16)
    part2[...] = (
        (dot_nt(dkv_ext[:, :COLS], wdkv[0]) + dot_nt(dkv_ext[:, COLS:], wdkv[1]))
        .astype(BF16).reshape(NY + 1, SHARE, D)
    )
    copies = scatter_share(part2, part2_in)

    def rim2_copy(side, slot):
        return pltpu.make_async_remote_copy(
            src_ref=part2.at[NY, pl.ds(side * RIM, RIM), :], dst_ref=rim2_in.at[slot],
            send_sem=rim2_send.at[side], recv_sem=rim2_recv.at[slot],
            device_id=(lower[NY - 1], upper[0])[side], device_id_type=MESH,
        )

    rim2_copy(0, y).start()
    rim2_copy(1, y).start()

    dec[...] = (dot_tn(flat(w_c), flat(vbd_c)) + dot_tn(flat(w_r), flat(vbd_r))).astype(BF16)
    dq[...] = (dot_tn(flat(ds_c), flat(kbd_c)) + dot_tn(flat(ds_r), flat(kbd_r))).astype(BF16)

    store_grad(ga, 0, gn_t, dq[...])
    paira = send_pair(ga, raa)
    store_grad(g0, 0, dout_t, dec[...])
    pair0 = send_pair(g0, ra0)
    store_grad(g1, 0, sn_t, dkv_ext[...])
    pair1 = send_pair(g1, ra1)

    arrive(copies)
    share[...] = share_sum(part2, part2_in)

    def rim_sum():
        for c in range(NY):
            rim2_copy(0, c).wait_recv()
        total = rim2_in[0].astype(F32)
        for c in range(1, NY):
            total = total + rim2_in[c].astype(F32)
        return total

    @pl.when(y == 0)
    def _():
        share[:RIM, :] = share[:RIM, :] + rim_sum()

    @pl.when(y == NY - 1)
    def _():
        share[SHARE - RIM :, :] = share[SHARE - RIM :, :] + rim_sum()

    sgrad[...] = normalise_back(yhat, rstd_y, share[...])
    sg[y] = sgrad[...].astype(BF16)
    copies = gather_share(sg)
    arrive(paira)
    add_pair_z(ga, raa, hba)
    za = send_z(hba, rza)
    arrive(pair0)
    add_pair(g0, ra0, hb0)
    x0 = send_x(hb0, ry0, rb0)

    def grid_part(i, carry):
        rows = pl.ds(pl.multiple_of(i * 128, 128), 128)
        half_rows = pl.ds(pl.multiple_of(lax.rem(i, 2) * 128, 128), 128)
        half = lax.div(i, 2)
        value = dot_nt(dq[rows, :], wdq[...])
        first = jnp.mean(value, axis=-1, keepdims=True)
        second = jnp.mean(value * gn[rows, :].astype(F32), axis=-1, keepdims=True)
        lane = lax.broadcasted_iota(jnp.int32, (128, 128), 1)
        both = jnp.where(lane == 0, first, jnp.where(lane == 1, second, 0.0)).T
        gstat[i] = both[:8]
        for q in range(NY):
            gb[half, q, half_rows, :] = value[:, q * COLS : (q + 1) * COLS].astype(BF16)
        return carry

    lax.fori_loop(0, POINTS // 128, grid_part, 0)

    def send_grid(half):
        return [
            push(gb.at[half, lax.rem(y + d, NY)], gb_in.at[half, d - 1], y_peers[d - 1]) for d in range(1, NY)
        ]

    arrive(pair1)
    add_pair(g1, ra1, hb1)
    x1 = send_x(hb1, ry1, rb1)
    x0 = relay_x(*x0, hb0, ry0, rb0)

    arrive(copies)
    grid_copies = send_grid(0)
    x1 = relay_x(*x1, hb1, ry1, rb1)
    state_grad_b = sg[...].reshape(ROWS, D)
    da = dot_nt(state_grad_b, wpo[...]).astype(BF16)
    dpt[...] = dot_nt(vbd[...].reshape(HEADS * span, COLS), da).reshape(HEADS, span, ROWS)

    def window_back(h, carry):
        prob = pt[h]
        dprob = dpt[h]
        centre = jnp.sum(prob * dprob, axis=0, keepdims=True)
        dpt[h] = prob * (dprob - centre)
        return carry

    lax.fori_loop(0, HEADS, window_back, 0)
    dscore = dpt[...].astype(BF16).reshape(HEADS * span, ROWS)
    dk_ext = own_head(dot_nn(dscore, qp[...]), span) * FACTOR
    dv_ext = own_head(dot_nn(pt[...].astype(BF16).reshape(HEADS * span, ROWS), da), span)
    for which, ext in ((0, dk_ext), (1, dv_ext)):
        rounded = ext.astype(BF16)
        dkv3[:, which * COLS : (which + 1) * COLS] = rounded
        ring_out[0, which] = rounded[:ROWS]
        ring_out[1, which] = rounded[2 * ROWS :]
    ring_copies = [push(ring_out.at[0], ring_in.at[0], below), push(ring_out.at[1], ring_in.at[1], above)]
    settled = len(used)
    store_grad(g2, 0, mn_t, dkv3[...])
    pair2 = send_pair(g2, ra2)
    dqkv[:, :COLS] = (
        dot_tn(dscore, kbd[...].reshape(HEADS * span, COLS)) * FACTOR
    ).astype(BF16)
    mn_own_t[...] = mn_t[:, ROWS : 2 * ROWS]
    store_grad(gq, 0, mn_own_t, dqkv[:, :COLS])
    pairq = send_pair(gq, raq)
    sg_t[...] = state_grad_b.T
    store_grad(g3, 0, sg_t, attended[...])
    pair3 = send_pair(g3, ra3)

    arrive(pair2)
    add_pair(g2, ra2, hb2)
    x2 = send_x_direct(hb2, ry2, rb2)
    arrive(pairq)
    add_pair_z(gq, raq, hbq)
    zq = send_z(hbq, rzq)
    arrive(pair3)
    add_pair(g3, ra3, hb3)
    x3 = send_x_direct(hb3, ry3, rb3)

    arrive(ring_copies)
    for which, ext in ((0, dk_ext), (1, dv_ext)):
        total = ext[ROWS : 2 * ROWS] + ring_in[0, which].astype(F32) + ring_in[1, which].astype(F32)
        dqkv[:, (which + 1) * COLS : (which + 2) * COLS] = total.astype(BF16)
    part3[...] = (
        (
            dot_nt(dqkv[:, :COLS], wqkv[0])
            + dot_nt(dqkv[:, COLS : 2 * COLS], wqkv[1])
            + dot_nt(dqkv[:, 2 * COLS :], wqkv[2])
        ).astype(BF16).reshape(NY, SHARE, D)
    )
    copies = scatter_share(part3, part3_in)

    arrive(copies)
    own_x = xhat[own_rows, :]
    centred, rstd_own = normalise(mesh_v[own_rows, :])
    result = sgrad[...] + normalise_back(own_x, rstd_own, share_sum(part3, part3_in))
    back[y] = result.astype(BF16)
    back_copies = gather_share(back)
    grid_copies += send_grid(1)
    for d in range(1, NY):
        grid_copies.append(push(gstat, gstat_in.at[d - 1], y_peers[d - 1]))

    arrive(za)
    add_z(hba, rza, hca)
    xa = send_x_last(hca, rxa)
    arrive(x0)
    add_x(hb0, rb0, hc0)
    z0 = send_z(hc0, rc0)
    arrive(x1)
    add_x(hb1, rb1, hc1)
    z1 = send_z(hc1, rc1)

    for copy in used[:settled]:
        copy.wait_send()
    arrive(x2)
    add_x_direct(hb2, ry2, rb2, hc2)
    z2 = send_z(hc2, rc2)
    arrive(zq)
    add_z(hbq, rzq, hcq)
    xq = send_x_last(hcq, rxq)
    arrive(x3)
    add_x_direct(hb3, ry3, rb3, hc3)
    z3 = send_z(hc3, rc3)

    arrive(grid_copies)
    columns = pl.ds(pl.multiple_of(y * COLS, COLS), COLS)

    def grid_final(i, carry):
        rows = pl.ds(pl.multiple_of(i * 128, 128), 128)
        stat = gstat[i]
        half_rows = pl.ds(pl.multiple_of(lax.rem(i, 2) * 128, 128), 128)
        half = lax.div(i, 2)
        value = gb[half, y, half_rows, :].astype(F32)
        for d in range(NY - 1):
            stat = stat + gstat_in[d, i]
            value = value + gb_in[half, d, half_rows, :].astype(F32)
        stat = jnp.concatenate([stat, jnp.zeros((120, 128), F32)], axis=0).T
        change = value - stat[:, 0:1] - gn[rows, columns].astype(F32) * stat[:, 1:2]
        out_grid[rows, :] = (dout_v[rows, columns].astype(F32) + grstd[rows, 0:1] * change).astype(BF16)
        return carry

    lax.fori_loop(0, POINTS // 128, grid_final, 0)
    arrive(back_copies)
    out_mesh[...] = back[...].reshape(ROWS, D)

    arrive(z0)
    out_do[...] = total_z(hc0, rc0)
    arrive(xa)
    out_dq[...] = total_x(hca, rxa)
    arrive(z1)
    total = total_z(hc1, rc1)
    out_dkv[0] = total[:PART]
    out_dkv[1] = total[PART:]
    arrive(z2)
    total = total_z(hc2, rc2)
    out_qkv[1] = total[:PART]
    out_qkv[2] = total[PART:]
    arrive(xq)
    out_qkv[0] = total_x(hcq, rxq)
    arrive(z3)
    out_po[...] = total_z(hc3, rc3)
    rim2_copy(0, 0).wait_send()
    rim2_copy(1, 0).wait_send()

    @pl.when((y == 0) | (y == NY - 1))
    def _():
        for c in range(NY):
            rim_copy(c, 0).wait_send()

    for copy in used[settled:]:
        copy.wait_send()


def copy_out(*refs):
    count = len(refs) // 2
    for source, target in zip(refs[:count], refs[count:]):
        target[...] = source[...]


def body(
    mesh_node_state, grid_state, d_out, neighbours, edge_count, w_proc_qkv, w_proc_out, w_dec_q, w_dec_kv, w_dec_out
):
    span = 3 * ROWS
    v = pltpu.VMEM

    def reduce_scratch(make):
        return [make(n * PART) for n in GROUPS]

    scratch = [
        v((ROWS, D), BF16), v((POINTS, D), BF16), v((POINTS, D), BF16), v((EDGES, POINTS), jnp.int32),
        v((1, POINTS), jnp.int32), v((3, D, COLS), BF16), v((COLS, D), BF16), v((D, COLS), BF16),
        v((2, D, COLS), BF16), v((COLS, D), BF16),
        v((ROWS, D), F32), v((3, ROWS, D), BF16), v((D, span), BF16), v((D, ROWS), BF16), v((D, ROWS + 2 * RIM), BF16), v((D, ROWS), BF16), v((3, 2, ROWS, COLS), BF16), v((ROWS, COLS), BF16),
        v((HEADS, span, COLS), BF16), v((HEADS, span, COLS), BF16), v((HEADS, span, ROWS), F32),
        v((HEADS, span, ROWS), F32), v((ROWS, COLS), BF16),
        v((NY, SHARE, D), BF16), v((NY - 1, SHARE, D), BF16), v((NY + 1, SHARE, D), BF16), v((POINTS, D), BF16),
        v((D, POINTS), BF16), v((D, POINTS), BF16), v((POINTS, 128), F32), v((POINTS, COLS), BF16),
        v((POINTS, COLS), BF16),
        v((2, ROWS + 2 * RIM, COLS), BF16),
        v((HEADS, ROWS, COLS), BF16), v((HEADS, ROWS, COLS), BF16),
        v((HEADS, 2 * RIM, COLS), BF16), v((HEADS, 2 * RIM, COLS), BF16),
        v((ROWS, POINTS), F32), v((2 * RIM, POINTS), F32),
        v((HEADS, ROWS, POINTS), F32), v((HEADS, 2 * RIM, POINTS), F32),
        v((HEADS, ROWS, POINTS), F32), v((HEADS, 2 * RIM, POINTS), F32),
        v((HEADS, ROWS, POINTS), BF16), v((HEADS, 2 * RIM, POINTS), BF16),
        v((HEADS, ROWS, POINTS), BF16), v((HEADS, 2 * RIM, POINTS), BF16),
        v((ROWS + 2 * RIM, 2 * COLS), BF16),
        v((POINTS, COLS), BF16), v((POINTS, COLS), BF16), v((2, NY, POINTS // 2, COLS), BF16),
        v((2, NY - 1, POINTS // 2, COLS), BF16), v((POINTS // 128, 8, 128), F32), v((NY - 1, POINTS // 128, 8, 128), F32),
        v((NY + 1, SHARE, D), BF16), v((NY - 1, SHARE, D), BF16), v((NY, RIM, D), BF16), v((SHARE, D), F32),
        v((SHARE, D), F32), v((NY, SHARE, D), BF16),
        v((2, 2, ROWS, COLS), BF16), v((2, 2, ROWS, COLS), BF16),
        v((span, 2 * COLS), BF16), v((ROWS, 3 * COLS), BF16),
        v((NY, SHARE, D), BF16), v((NY - 1, SHARE, D), BF16), v((NY, SHARE, D), BF16),
    ]
    scratch += reduce_scratch(lambda r: v((NC, NX, NZ, r, COLS), BF16))
    scratch += reduce_scratch(lambda r: v((NX, NZ, r, COLS), BF16))
    scratch += reduce_scratch(lambda r: v((NX, NZ, r, COLS), BF16))
    scratch += reduce_scratch(lambda r: v((2, HALF, r, COLS), BF16))[:2]
    scratch += reduce_scratch(lambda r: v((NZ, r, COLS), BF16))[2:]
    scratch += reduce_scratch(lambda r: v((2, NZ, r, COLS), BF16))
    scratch += reduce_scratch(lambda r: v((NZ, r, COLS), BF16))
    scratch += reduce_scratch(lambda r: v((NZ - 1, r, COLS), BF16))
    chunk = (PART, COLS)
    for lead in ((NC, NX, NZ), (NX, NZ), (NZ, NX), (NZ - 1, NX), (NX,), (NX - 1,)):
        scratch += [v(lead + chunk, BF16), v(lead + chunk, BF16)]
    scratch += [
        pltpu.SemaphoreType.DMA((10,)), pltpu.SemaphoreType.DMA((REMOTE,)), pltpu.SemaphoreType.DMA((REMOTE,)),
        pltpu.SemaphoreType.DMA((NY,)), pltpu.SemaphoreType.DMA((2,)), pltpu.SemaphoreType.DMA((2,)),
        pltpu.SemaphoreType.DMA((NY,)),
    ]
    shapes = (
        ((ROWS, D), BF16), ((POINTS, COLS), BF16), ((3, PART, COLS), F32), ((PART, COLS), F32),
        ((PART, COLS), F32), ((2, PART, COLS), F32), ((PART, COLS), F32),
    )
    results = pl.pallas_call(
        kernel,
        out_shape=[jax.ShapeDtypeStruct(shape, kind) for shape, kind in shapes],
        in_specs=[pl.BlockSpec(memory_space=pl.ANY)] * 10,
        out_specs=[pl.BlockSpec(memory_space=pltpu.VMEM)] * 7,
        scratch_shapes=scratch,
        compiler_params=pltpu.CompilerParams(
            collective_id=0, has_side_effects=True, vmem_limit_bytes=56 * 2**20
        ),
    )(
        mesh_node_state, grid_state, d_out, neighbours.T, edge_count.reshape(1, POINTS),
        w_proc_qkv, w_proc_out, w_dec_q, w_dec_kv, w_dec_out,
    )
    mesh_grad, grid_grad, g_qkv, g_po, g_dq, g_dkv, g_do = pl.pallas_call(
        copy_out,
        out_shape=[jax.ShapeDtypeStruct(shape, kind) for shape, kind in shapes],
        in_specs=[pl.BlockSpec(memory_space=pltpu.VMEM)] * 7,
        out_specs=[pl.BlockSpec(memory_space=pltpu.VMEM)] * 7,
    )(*results)
    return mesh_grad, grid_grad, g_qkv, g_po.T, g_dq, g_dkv, g_do.T


def solution(mesh):
    placed = (
        P("band", None), P("band", None), P("band", None), P("band", None), P("band"),
        P(None, None, "chan"), P("chan", None), P(None, "chan"), P(None, None, "chan"), P("chan", None),
    )
    return jax.shard_map(
        body,
        mesh=mesh,
        in_specs=placed,
        out_specs=(
            P("band", None), P("band", "chan"), P(None, "band", "chan"), P("chan", "band"),
            P("band", "chan"), P(None, "band", "chan"), P("chan", "band"),
        ),
        check_vma=False,
    )
```
